32 devices in a mesh: wave: 8 (over z, x), tile: 4 (over y, core).
Axes of the slice: x: 2, y: 2, z: 4, core: 2. Of those that a mesh axis runs over, the one named last changes fastest.
Arguments:
- scene: float32 [32, 1024, 1024], P('wave', 'tile'), may hold values from -6 to 6
- bank: float32 [32, 8, 8, 128, 128], P('wave', 'tile'), may hold values from -0.046875 to 0.046875
- psf_index: int32 [8, 8, 4], P('tile'), may hold values from 0 to 63, as said below
- psf_weight: int32 [8, 8, 4], P('tile'), may hold values from 1 to 32768
- response: float32 [3, 32], replicated, may hold values from -1 to 1
Outputs:
- colour: float32 [3, 1024, 1024], P(None, ('tile', 'wave'))
The draws below stay inside these ranges and needn't reach their ends.
Inputs may be any that keep to these rules, and one draw needn't show every extreme that they name: Entry k of tile (r, c) names the field point (psf_index // 8, psf_index % 8), which lies at most one tile row and at most one tile column from (r, c); entry 0 names (r, c) itself.
All inputs are finite; a program needn't handle non-finite values.
Results may differ from the reference program's by a relative error of at most 0.0001.
Values sent between devices are 32-bit elements; how exact they have to be, the bound alone decides.
A program may use at most 64 MiB of HBM per device.

```python
import jax
import jax.numpy as jnp
from jax import lax

P_SIZE = 128
WAVES = 32
K = 4
GC = 8
GR = 8
H = 1024
W = 1024


def draw_psf_index(key, part):
    key_rows, key_cols = jax.random.split(key)
    row_ids = lax.iota(jnp.int32, GR)[:, None, None]
    col_ids = lax.iota(jnp.int32, GC)[None, :, None]
    first_entry = (lax.iota(jnp.int32, K) == 0)[None, None, :]
    row_step = jax.random.randint(key_rows, (GR, GC, K), -1, 2)
    col_step = jax.random.randint(key_cols, (GR, GC, K), -1, 2)
    row_step = jnp.where(first_entry, 0, row_step)
    col_step = jnp.where(first_entry, 0, col_step)
    row_pick = jnp.clip(row_ids + row_step, 0, GR - 1)
    col_pick = jnp.clip(col_ids + col_step, 0, GC - 1)
    return (row_pick * GC + col_pick).astype(jnp.int32)


def set_ends(result, own_key, smallest, top_value):
    place = [jax.random.randint(jax.random.fold_in(own_key, axis), (), 0, length) for axis, length in enumerate(result.shape)]
    longest = result.shape.index(max(result.shape))
    neighbour = place[:longest] + [(place[longest] + 1) % result.shape[longest]] + place[longest + 1:]
    return result.at[tuple(place)].set(smallest).at[tuple(neighbour)].set(top_value)


def levels(stream_key, extent, cuts, least, high):
    loudness = 1.0
    for dim, blocks in cuts:
        draws = jax.random.uniform(jax.random.fold_in(jax.random.fold_in(stream_key, 6), dim), (blocks,), jnp.float32, least / len(cuts), high / len(cuts))
        loudness = loudness * jnp.repeat(jnp.exp(draws), extent[dim] // blocks).reshape((-1,) + (1,) * (len(extent) - 1 - dim))
    return loudness


def normal_values(key, dims, spread, reach, shards=(), dtype=jnp.bfloat16):
    result = spread * jax.random.normal(key, dims, jnp.float32)
    if shards:
        result = result * levels(key, dims, shards, -0.22, 0.18)
    return jnp.clip(result, -reach, reach).astype(dtype)


def setup_inputs(seed: int = 0) -> dict:
    key_list = jax.random.split(jax.random.key(seed), 6)
    return {
        "scene": normal_values(key_list[0], (WAVES, H, W), 1.0, 6.0, ((0, 8), (1, 4)), jnp.float32),
        "bank": normal_values(key_list[1], (WAVES, GR, GC, P_SIZE, P_SIZE), (P_SIZE * P_SIZE) ** -0.5, 0.046875, ((0, 8), (1, 4)), jnp.float32),
        "psf_index": draw_psf_index(jax.random.fold_in(key_list[5], 71), 0),
        "psf_weight": set_ends(jax.random.randint(key_list[3], (GR, GC, K), 1, 32769), jax.random.fold_in(key_list[3], 1), 1, 32768).astype(jnp.int32),
        "response": normal_values(key_list[4], (3, WAVES), WAVES ** -0.5, 1.0, (), jnp.float32),
    }


def blur_wave(scene_plane, bank_plane, psf_index, psf_weight):
    tile_rows, tile_cols, side = bank_plane.shape[0], bank_plane.shape[1], bank_plane.shape[-1]
    length = 2 * side
    margin = side // 2
    flat_bank = bank_plane.reshape(tile_rows * tile_cols, side, side)
    fraction = psf_weight.astype(jnp.float32) / 65536.0
    psf_set = jnp.einsum('rck,rckab->rcab', fraction, flat_bank[psf_index], precision=lax.Precision.HIGHEST)
    tile_set = scene_plane.reshape(tile_rows, side, tile_cols, side).transpose(0, 2, 1, 3)
    scene_spec = jnp.fft.rfft2(tile_set, s=(length, length))
    psf_spec = jnp.fft.rfft2(psf_set, s=(length, length))
    circular = jnp.fft.irfft2(scene_spec * psf_spec, s=(length, length))
    left_half = jnp.pad(circular[..., :side], ((0, 0), (0, 1), (0, 0), (0, 0)))
    right_half = jnp.pad(circular[..., side:], ((0, 0), (1, 0), (0, 0), (0, 0)))
    columns = (left_half + right_half).transpose(0, 2, 1, 3).reshape(tile_rows, length, (tile_cols + 1) * side)
    columns = columns[:, :, margin:margin + tile_cols * side]
    top_half = jnp.pad(columns[:, :side], ((0, 1), (0, 0), (0, 0)))
    bottom_half = jnp.pad(columns[:, side:], ((1, 0), (0, 0), (0, 0)))
    summed = (top_half + bottom_half).reshape((tile_rows + 1) * side, tile_cols * side)
    return summed[margin:margin + tile_rows * side]


def reference(scene, bank, psf_index, psf_weight, response):
    def accumulate(total, inputs):
        scene_plane, bank_plane, weights_now = inputs
        blurred = blur_wave(scene_plane, bank_plane, psf_index, psf_weight)
        return total + weights_now[:, None, None] * blurred[None], None

    start = jnp.zeros((3, scene.shape[1], scene.shape[2]), jnp.float32)
    colour, unused = lax.scan(accumulate, start, (scene, bank, response.T))
    return colour
```

```python
import functools

import jax
import jax.numpy as jnp
import ml_dtypes
import numpy as np
from jax import lax
from jax.experimental import pallas as pl
from jax.experimental.pallas import tpu as pltpu
from jax.sharding import PartitionSpec as P

CHUNKS = 2
CHUNK_ROWS = 16
VMEM_BYTES = 56 * 1024 * 1024


def halves(table):
    high = table.astype(ml_dtypes.bfloat16)
    low = (table - high.astype(np.float64)).astype(ml_dtypes.bfloat16)
    return high, low


def left_factor(table):
    high, low = halves(table)
    return np.concatenate([high, high, low], axis=1)


def right_factor(table):
    high, low = halves(table)
    return np.concatenate([high, high, low], axis=0)


def tables(side):
    length = 2 * side
    odd = 2 * np.arange(side)[:, None] + 1
    angle = np.pi * (odd * np.arange(length)[None, :] % (2 * length)) / length
    cosine, sine = np.cos(angle), np.sin(angle)
    rows_in = np.concatenate([cosine[:, :side], -sine[:, :side]], axis=0)
    cols_in = np.concatenate([cosine[:, :side].T, sine[:, :side].T], axis=1)
    cols_out = np.concatenate([cosine, sine], axis=0)
    rows_out = np.concatenate([cosine.T, -sine.T], axis=1) * (2.0 / (length * length))
    return left_factor(rows_in), right_factor(cols_in), right_factor(cols_out), left_factor(rows_out)


def split(values):
    high = values.astype(jnp.bfloat16)
    low = (values - high.astype(jnp.float32)).astype(jnp.bfloat16)
    return high, low


def dot(left, right):
    return jnp.dot(left, right, preferred_element_type=jnp.float32)


def put_rows(out_ref, values, side, lanes):
    high, low = split(values)
    out_ref[0:side, lanes] = high
    out_ref[side : 2 * side, lanes] = low
    out_ref[2 * side : 3 * side, lanes] = high


def put_cols(out_ref, values, width, rows):
    high, low = split(values)
    out_ref[rows, 0:width] = high
    out_ref[rows, width : 2 * width] = low
    out_ref[rows, 2 * width : 3 * width] = high


def scene_kernel(side, tile_cols, rows_ref, cols_ref, scene_ref, out_ref, lifted, mid, spec):
    put_rows(lifted, scene_ref[0], side, slice(None))
    first = dot(rows_ref[...], lifted[...])
    for c in range(tile_cols):
        put_cols(mid, first[:, c * side : (c + 1) * side], side, slice(2 * c * side, 2 * (c + 1) * side))
    spec[...] = dot(mid[...], cols_ref[...])
    for c in range(tile_cols):
        top = 2 * c * side
        a = spec[top : top + side, 0:side]
        b = spec[top : top + side, side : 2 * side]
        d = spec[top + side : top + 2 * side, 0:side]
        e = spec[top + side : top + 2 * side, side : 2 * side]
        out_ref[0, 0, c, 0:side, 0:side] = a + e
        out_ref[0, 0, c, side : 2 * side, 0:side] = d - b
        out_ref[0, 0, c, 0:side, side : 2 * side] = a - e
        out_ref[0, 0, c, side : 2 * side, side : 2 * side] = d + b


def scene_spectra(scene, row_table, col_table, side):
    waves, strip, width = scene.shape
    tile_rows, tile_cols = strip // side, width // side
    whole = lambda w, r: (0, 0)
    return pl.pallas_call(
        functools.partial(scene_kernel, side, tile_cols),
        grid=(waves, tile_rows),
        in_specs=[
            pl.BlockSpec(row_table.shape, whole),
            pl.BlockSpec(col_table.shape, whole),
            pl.BlockSpec((1, side, width), lambda w, r: (w, r, 0)),
        ],
        out_specs=pl.BlockSpec((1, 1, tile_cols, 2 * side, 2 * side), lambda w, r: (w, r, 0, 0, 0)),
        out_shape=jax.ShapeDtypeStruct((waves, tile_rows, tile_cols, 2 * side, 2 * side), jnp.float32),
        scratch_shapes=[
            pltpu.VMEM((3 * side, width), jnp.bfloat16),
            pltpu.VMEM((2 * side * tile_cols, 3 * side), jnp.bfloat16),
            pltpu.VMEM((2 * side * tile_cols, 2 * side), jnp.float32),
        ],
        compiler_params=pltpu.CompilerParams(vmem_limit_bytes=VMEM_BYTES),
        cost_estimate=pl.CostEstimate(
            flops=waves * tile_rows * tile_cols * 12 * 2 * side**3,
            bytes_accessed=5 * 4 * waves * strip * width,
            transcendentals=0,
        ),
        name="scene_spectra",
    )(row_table, col_table, scene)


def colour_kernel(
    dims,
    slot_ref,
    weight_ref,
    response_ref,
    rows_in,
    cols_in,
    cols_out,
    rows_out,
    spec_ref,
    own_ref,
    above_ref,
    below_ref,
    carry_in,
    out_ref,
    carry_out,
    extended,
    carry,
    psf_lifted,
    psf_mid,
    psf_spec,
    mixed,
    back,
    copied,
):
    first_col, count, tile_rows, tile_cols, entries, side, waves, channels = dims
    step = pl.program_id(0)
    length = 2 * side

    @pl.when(step == 0)
    def _():
        inner = tile_rows * tile_cols
        copies = [
            pltpu.make_async_copy(above_ref, extended.at[:, pl.ds(0, tile_cols)], copied.at[0]),
            pltpu.make_async_copy(own_ref, extended.at[:, pl.ds(tile_cols, inner)], copied.at[1]),
            pltpu.make_async_copy(below_ref, extended.at[:, pl.ds(tile_cols + inner, tile_cols)], copied.at[2]),
        ]
        for copy in copies:
            copy.start()
        carry[...] = carry_in[...]
        for copy in copies:
            copy.wait()

    @pl.when(step < count)
    def _():
        for r in range(tile_rows):
            place = (r * tile_cols + first_col + step) * entries
            for w in range(waves):
                psf = weight_ref[place] * extended[w, slot_ref[place]]
                for k in range(1, entries):
                    psf = psf + weight_ref[place + k] * extended[w, slot_ref[place + k]]
                put_rows(psf_lifted, psf, side, slice(w * side, (w + 1) * side))
            first = dot(rows_in[...], psf_lifted[...])
            for w in range(waves):
                put_cols(
                    psf_mid, first[:, w * side : (w + 1) * side], side, slice(w * length, (w + 1) * length)
                )
            psf_spec[...] = dot(psf_mid[...], cols_in[...])

            def some_rows(index, state):
                start = pl.multiple_of(index * CHUNK_ROWS, CHUNK_ROWS)
                upper = pl.ds(start, CHUNK_ROWS)
                lower = pl.ds(start + side, CHUNK_ROWS)
                left, right = slice(0, side), slice(side, length)
                sums = [None] * channels
                for w in range(waves):
                    p_upper = pl.ds(start + w * length, CHUNK_ROWS)
                    p_lower = pl.ds(start + w * length + side, CHUNK_ROWS)
                    a, b = psf_spec[p_upper, left], psf_spec[p_upper, right]
                    d, e = psf_spec[p_lower, left], psf_spec[p_lower, right]
                    p1r, p1i, p2r, p2i = a + e, d - b, a - e, d + b
                    s1r, s1i = spec_ref[w, r, 0, upper, left], spec_ref[w, r, 0, lower, left]
                    s2r, s2i = spec_ref[w, r, 0, upper, right], spec_ref[w, r, 0, lower, right]
                    q1r, q1i = s1r * p1r - s1i * p1i, s1r * p1i + s1i * p1r
                    q2r, q2i = s2r * p2r - s2i * p2i, s2r * p2i + s2i * p2r
                    parts = (q1r + q2r, q2i - q1i, q1i + q2i, q1r - q2r)
                    for ch in range(channels):
                        gain = response_ref[ch, w]
                        terms = [gain * part for part in parts]
                        sums[ch] = terms if w == 0 else [old + new for old, new in zip(sums[ch], terms)]
                for ch in range(channels):
                    for j, rows in ((0, pl.ds(start + ch * length, CHUNK_ROWS)), (2, pl.ds(start + ch * length + side, CHUNK_ROWS))):
                        for h in range(2):
                            high, low = split(sums[ch][j + h])
                            mixed[rows, h * side : (h + 1) * side] = high
                            mixed[rows, length + h * side : length + (h + 1) * side] = low
                            mixed[rows, 2 * length + h * side : 2 * length + (h + 1) * side] = high
                return state

            lax.fori_loop(0, side // CHUNK_ROWS, some_rows, 0)
            partial = dot(mixed[...], cols_out[...])
            for ch in range(channels):
                rows = slice(ch * length, (ch + 1) * length)
                lane = (r * channels + ch) * side
                block = partial[rows, 0:side] + carry[r, rows, :]
                put_rows(back, block, length, slice(lane, lane + side))
                carry[r, rows, :] = partial[rows, side:length]

    @pl.when(step >= count)
    def _():
        for r in range(tile_rows):
            for ch in range(channels):
                rows = slice(ch * length, (ch + 1) * length)
                lane = (r * channels + ch) * side
                put_rows(back, carry[r, rows, :], length, slice(lane, lane + side))

    light = dot(rows_out[...], back[...])
    for ch in range(channels):
        for r in range(tile_rows + 1):
            total = None
            if r < tile_rows:
                lane = (r * channels + ch) * side
                total = light[0:side, lane : lane + side]
            if r > 0:
                lane = ((r - 1) * channels + ch) * side
                low = light[side:length, lane : lane + side]
                total = low if total is None else total + low
            out_ref[ch, r * side : (r + 1) * side, :] = total

    @pl.when(step == pl.num_programs(0) - 1)
    def _():
        carry_out[...] = carry[...]


def colour_columns(spectra, own, above, below, slots, weights, response, carry, cols, side):
    row_in, col_in, col_out, row_out = tables(side)
    waves, tile_rows, tile_cols = spectra.shape[:3]
    channels = response.shape[0]
    length = 2 * side
    first_col, count = cols
    entries = slots.shape[0] // (tile_rows * tile_cols)
    steps = count + (1 if first_col + count == tile_cols else 0)
    dims = (first_col, count, tile_rows, tile_cols, entries, side, waves, channels)
    smem = pl.BlockSpec(memory_space=pltpu.SMEM)
    anywhere = pl.BlockSpec(memory_space=pl.ANY)
    whole = lambda c: (0, 0)
    return pl.pallas_call(
        functools.partial(colour_kernel, dims),
        grid=(steps,),
        in_specs=[
            smem,
            smem,
            smem,
            pl.BlockSpec(row_in.shape, whole),
            pl.BlockSpec(col_in.shape, whole),
            pl.BlockSpec(col_out.shape, whole),
            pl.BlockSpec(row_out.shape, whole),
            pl.BlockSpec(
                (waves, tile_rows, 1, length, length),
                lambda c: (0, 0, first_col + jnp.minimum(c, count - 1), 0, 0),
            ),
            anywhere,
            anywhere,
            anywhere,
            pl.BlockSpec(carry.shape, lambda c: (0, 0, 0)),
        ],
        out_specs=[
            pl.BlockSpec((channels, (tile_rows + 1) * side, side), lambda c: (0, 0, c)),
            pl.BlockSpec(carry.shape, lambda c: (0, 0, 0)),
        ],
        out_shape=[
            jax.ShapeDtypeStruct((channels, (tile_rows + 1) * side, steps * side), jnp.float32),
            jax.ShapeDtypeStruct(carry.shape, jnp.float32),
        ],
        scratch_shapes=[
            pltpu.VMEM((waves, (tile_rows + 2) * tile_cols, side, side), jnp.float32),
            pltpu.VMEM(carry.shape, jnp.float32),
            pltpu.VMEM((3 * side, waves * side), jnp.bfloat16),
            pltpu.VMEM((waves * length, 3 * side), jnp.bfloat16),
            pltpu.VMEM((waves * length, length), jnp.float32),
            pltpu.VMEM((channels * length, 3 * length), jnp.bfloat16),
            pltpu.VMEM((3 * length, tile_rows * channels * side), jnp.bfloat16),
            pltpu.SemaphoreType.DMA((3,)),
        ],
        compiler_params=pltpu.CompilerParams(vmem_limit_bytes=VMEM_BYTES),
        cost_estimate=pl.CostEstimate(
            flops=count * tile_rows * (waves * 12 + channels * 36) * 2 * side**3,
            bytes_accessed=4 * waves * tile_rows * count * length * length,
            transcendentals=0,
        ),
        name="colour_columns",
    )(slots, weights, response, row_in, col_in, col_out, row_out, spectra, own, above, below, carry)


def shifted(values, axis, by):
    size = lax.axis_size(axis)
    return lax.ppermute(values, axis, [(i, i + by) for i in range(size) if 0 <= i + by < size])


def scatter_sum(values, axis, x_first):
    size = lax.axis_size(axis)
    bits = size.bit_length() - 1
    channels, rows, columns = values.shape
    me = lax.axis_index(axis)
    values = values.reshape((channels,) + (2,) * bits + (rows // size, columns))
    left = list(range(bits - 1, -1, -1))
    order = list(range(bits)) if x_first else list(range(1, bits)) + [0]
    for bit in order:
        dim = 1 + left.index(bit)
        mine = (me >> bit) & 1
        keep = lax.dynamic_index_in_dim(values, mine, dim, keepdims=False)
        give = lax.dynamic_index_in_dim(values, 1 - mine, dim, keepdims=False)
        values = keep + lax.ppermute(give, axis, [(i, i ^ (1 << bit)) for i in range(size)])
        left.remove(bit)
    return values


def per_device(scene, bank, psf_index, psf_weight, response):
    waves, tile_rows, tile_cols, side = bank.shape[:4]
    entries = psf_index.shape[-1]
    margin = side // 2
    strip = tile_rows * side
    channels = response.shape[0]
    above = shifted(bank[:, tile_rows - 1], "tile", 1)
    below = shifted(bank[:, 0], "tile", -1)
    own = bank.reshape(waves, tile_rows * tile_cols, side, side)
    first_slot = (lax.axis_index("tile") * tile_rows - 1) * tile_cols
    slots = (psf_index - first_slot).reshape(tile_rows * tile_cols * entries)
    weights = (psf_weight.astype(jnp.float32) / 65536.0).reshape(tile_rows * tile_cols * entries)
    own_response = lax.dynamic_slice_in_dim(response, lax.axis_index("wave") * waves, waves, 1)
    row_in, col_in, _, _ = tables(side)
    spectra = scene_spectra(scene, row_in, col_in, side)
    carry = jnp.zeros((tile_rows, channels * 2 * side, side), jnp.float32)
    count = tile_cols // CHUNKS
    pieces = []
    for g in range(CHUNKS):
        light, carry = colour_columns(
            spectra, own, above, below, slots, weights, own_response, carry, (g * count, count), side
        )
        from_above = shifted(light[:, strip + margin :], "tile", 1)
        from_below = shifted(light[:, :margin], "tile", -1)
        middle = light[:, margin : margin + strip]
        middle = jnp.concatenate(
            [middle[:, :margin] + from_above, middle[:, margin:-margin], middle[:, -margin:] + from_below], axis=1
        )
        pieces.append(scatter_sum(middle, "wave", g % 2 == 0))
    colour = jnp.concatenate(pieces, axis=2)
    return colour[:, :, margin : margin + tile_cols * side]


def solution(mesh):
    in_specs = (
        P("wave", "tile", None),
        P("wave", "tile", None, None, None),
        P("tile", None, None),
        P("tile", None, None),
        P(),
    )
    out_specs = P(None, ("tile", "wave"), None)
    return jax.shard_map(
        per_device, mesh=mesh, in_specs=in_specs, out_specs=out_specs, check_vma=False
    )
```

```python
import functools

import jax
import jax.numpy as jnp
import ml_dtypes
import numpy as np
from jax import lax
from jax.experimental import pallas as pl
from jax.experimental.pallas import tpu as pltpu
from jax.sharding import PartitionSpec as P

CHUNK_ROWS = 16
VMEM_BYTES = 56 * 1024 * 1024


def halves(table):
    high = table.astype(ml_dtypes.bfloat16)
    low = (table - high.astype(np.float64)).astype(ml_dtypes.bfloat16)
    return high, low


def left_factor(table):
    high, low = halves(table)
    return np.concatenate([high, high, low], axis=1)


def right_factor(table):
    high, low = halves(table)
    return np.concatenate([high, high, low], axis=0)


def tables(side):
    length = 2 * side
    odd = 2 * np.arange(side)[:, None] + 1
    angle = np.pi * (odd * np.arange(length)[None, :] % (2 * length)) / length
    cosine, sine = np.cos(angle), np.sin(angle)
    rows_in = np.concatenate([cosine[:, :side], -sine[:, :side]], axis=0)
    cols_in = np.concatenate([cosine[:, :side].T, sine[:, :side].T], axis=1)
    cols_out = np.concatenate([cosine, sine], axis=0)
    rows_out = np.concatenate([cosine.T, -sine.T], axis=1) * (2.0 / (length * length))
    return left_factor(rows_in), right_factor(cols_in), right_factor(cols_out), left_factor(rows_out)


def split(values):
    high = values.astype(jnp.bfloat16)
    low = (values - high.astype(jnp.float32)).astype(jnp.bfloat16)
    return high, low


def dot(left, right):
    return jnp.dot(left, right, preferred_element_type=jnp.float32)


def put_rows(out_ref, values, side, lanes):
    high, low = split(values)
    out_ref[0:side, lanes] = high
    out_ref[side : 2 * side, lanes] = low
    out_ref[2 * side : 3 * side, lanes] = high


def put_cols(out_ref, values, width, rows):
    high, low = split(values)
    out_ref[rows, 0:width] = high
    out_ref[rows, width : 2 * width] = low
    out_ref[rows, 2 * width : 3 * width] = high


def camera_kernel(
    dims,
    weight_ref,
    response_ref,
    rows_in,
    cols_in,
    cols_out,
    rows_out,
    scene_ref,
    bank_ref,
    out_ref,
    above,
    below,
    carry,
    lifted,
    lift_mid,
    scene_spec,
    psf_spec,
    mixed,
    back,
    light,
    light_above,
    light_below,
    middle,
    got_low,
    part,
    got_high,
    bank_sent,
    bank_got,
    light_sent,
    light_got,
    low_sent,
    low_got,
    high_sent,
    high_got,
):
    tile_count, low_count, high_count, tile_rows, tile_cols, side, waves, channels = dims
    step = pl.program_id(0)
    length, margin, strip = 2 * side, side // 2, tile_rows * side
    slab = strip // (low_count * high_count)
    blocks = tile_cols + 1
    tile, wave = lax.axis_index("tile"), lax.axis_index("wave")
    low, high = lax.rem(wave, low_count), lax.div(wave, low_count)
    has_above, has_below = tile > 0, tile < tile_count - 1
    tile_above = lax.rem(tile + tile_count - 1, tile_count)
    tile_below = lax.rem(tile + 1, tile_count)

    def remote(src, dst, sent, got, axis, index):
        return pltpu.make_async_remote_copy(
            src_ref=src,
            dst_ref=dst,
            send_sem=sent,
            recv_sem=got,
            device_id={axis: index},
            device_id_type=pl.DeviceIdType.MESH,
        )

    def bank_down(c):
        return remote(
            bank_ref.at[:, tile_rows - 1, c], above.at[c], bank_sent.at[0, c], bank_got.at[0, c], "tile", tile_below
        )

    def bank_up(c):
        return remote(bank_ref.at[:, 0, c], below.at[c], bank_sent.at[1, c], bank_got.at[1, c], "tile", tile_above)

    def light_down(b):
        return remote(
            light.at[b, :, pl.ds(strip + margin, margin)],
            light_above.at[b],
            light_sent.at[0, b],
            light_got.at[0, b],
            "tile",
            tile_below,
        )

    def light_up(b):
        return remote(
            light.at[b, :, pl.ds(0, margin)], light_below.at[b], light_sent.at[1, b], light_got.at[1, b], "tile", tile_above
        )

    def start_pair(down, up):
        @pl.when(has_below)
        def _():
            down.start()

        @pl.when(has_above)
        def _():
            up.start()

    def wait_pair(down, up):
        @pl.when(has_below)
        def _():
            down.wait_send()
            up.wait_recv()

        @pl.when(has_above)
        def _():
            up.wait_send()
            down.wait_recv()

    def low_peer(d):
        return lax.rem(low + d, low_count)

    def high_peer(d):
        return lax.rem(high + d, high_count)

    def to_low(b, d):
        peer = low_peer(d)
        return remote(
            middle.at[b, peer],
            got_low.at[b, d - 1],
            low_sent.at[b, d - 1],
            low_got.at[b, d - 1],
            "wave",
            high * low_count + peer,
        )

    def to_high(b, d):
        peer = high_peer(d)
        return remote(
            part.at[b, peer],
            got_high.at[b, d - 1],
            high_sent.at[b, d - 1],
            high_got.at[b, d - 1],
            "wave",
            peer * low_count + low,
        )

    @pl.when(step == 0)
    def _():
        barrier = pltpu.get_barrier_semaphore()

        def greet(axis, index):
            pl.semaphore_signal(barrier, inc=1, device_id={axis: index}, device_id_type=pl.DeviceIdType.MESH)

        for d in range(1, low_count):
            greet("wave", high * low_count + low_peer(d))
        for d in range(1, high_count):
            greet("wave", high_peer(d) * low_count + low)

        @pl.when(has_above)
        def _():
            greet("tile", tile_above)

        @pl.when(has_below)
        def _():
            greet("tile", tile_below)

        others = low_count + high_count - 2
        pl.semaphore_wait(barrier, others + has_above.astype(jnp.int32) + has_below.astype(jnp.int32))
        for c in range(min(3, tile_cols)):
            start_pair(bank_down(c), bank_up(c))
        carry[...] = jnp.zeros_like(carry)

        @pl.when(jnp.logical_not(has_above))
        def _():
            above[...] = jnp.zeros_like(above)
            light_above[...] = jnp.zeros_like(light_above)

        @pl.when(jnp.logical_not(has_below))
        def _():
            below[...] = jnp.zeros_like(below)
            light_below[...] = jnp.zeros_like(light_below)

    @pl.when(jnp.logical_and(step > 0, step + 2 < tile_cols))
    def _():
        start_pair(bank_down(step + 2), bank_up(step + 2))

    def transform(spec):
        first = dot(rows_in[...], lifted[...])
        for t in range(tile_rows * waves):
            put_cols(lift_mid, first[:, t * side : (t + 1) * side], side, slice(t * length, (t + 1) * length))
        spec[...] = dot(lift_mid[...], cols_in[...])

    @pl.when(step < tile_cols)
    def _():
        for r in range(tile_rows):
            for w in range(waves):
                lane = (r * waves + w) * side
                put_rows(lifted, scene_ref[w, r * side : (r + 1) * side, :], side, slice(lane, lane + side))
        transform(scene_spec)

        @pl.when(step == 0)
        def _():
            wait_pair(bank_down(0), bank_up(0))

        @pl.when(step + 1 < tile_cols)
        def _():
            wait_pair(bank_down(step + 1), bank_up(step + 1))

        near = (jnp.maximum(step - 1, 0), step, jnp.minimum(step + 1, tile_cols - 1))
        for r in range(tile_rows):
            place = (r * tile_cols + step) * 9
            for w in range(waves):
                psf = None
                for i in range(3):
                    for j in range(3):
                        row = r + i - 1
                        if row < 0:
                            field = above[near[j], w]
                        elif row >= tile_rows:
                            field = below[near[j], w]
                        else:
                            field = bank_ref[w, row, near[j]]
                        term = weight_ref[place + 3 * i + j] * field
                        psf = term if psf is None else psf + term
                lane = (r * waves + w) * side
                put_rows(lifted, psf, side, slice(lane, lane + side))
        transform(psf_spec)

        def some_rows(r, index, state):
            start = pl.multiple_of(index * CHUNK_ROWS, CHUNK_ROWS)
            left, right = slice(0, side), slice(side, length)
            sums = [None] * channels
            for w in range(waves):
                upper = pl.ds(start + (r * waves + w) * length, CHUNK_ROWS)
                lower = pl.ds(start + (r * waves + w) * length + side, CHUNK_ROWS)
                a, b, d, e = psf_spec[upper, left], psf_spec[upper, right], psf_spec[lower, left], psf_spec[lower, right]
                p1r, p1i, p2r, p2i = a + e, d - b, a - e, d + b
                a, b, d, e = (
                    scene_spec[upper, left],
                    scene_spec[upper, right],
                    scene_spec[lower, left],
                    scene_spec[lower, right],
                )
                s1r, s1i, s2r, s2i = a + e, d - b, a - e, d + b
                q1r, q1i = s1r * p1r - s1i * p1i, s1r * p1i + s1i * p1r
                q2r, q2i = s2r * p2r - s2i * p2i, s2r * p2i + s2i * p2r
                parts = (q1r + q2r, q2i - q1i, q1i + q2i, q1r - q2r)
                for ch in range(channels):
                    gain = response_ref[ch, w]
                    terms = [gain * value for value in parts]
                    sums[ch] = terms if w == 0 else [old + new for old, new in zip(sums[ch], terms)]
            for ch in range(channels):
                top = start + (r * channels + ch) * length
                for j, rows in ((0, pl.ds(top, CHUNK_ROWS)), (2, pl.ds(top + side, CHUNK_ROWS))):
                    for h in range(2):
                        upper_bits, lower_bits = split(sums[ch][j + h])
                        mixed[rows, h * side : (h + 1) * side] = upper_bits
                        mixed[rows, length + h * side : length + (h + 1) * side] = lower_bits
                        mixed[rows, 2 * length + h * side : 2 * length + (h + 1) * side] = upper_bits
            return state

        for r in range(tile_rows):
            lax.fori_loop(0, side // CHUNK_ROWS, functools.partial(some_rows, r), 0)
        partial = dot(mixed[...], cols_out[...])
        for r in range(tile_rows):
            for ch in range(channels):
                rows = slice((r * channels + ch) * length, (r * channels + ch + 1) * length)
                lane = (r * channels + ch) * side
                put_rows(back, partial[rows, 0:side] + carry[rows, :], length, slice(lane, lane + side))
                carry[rows, :] = partial[rows, side:length]

    @pl.when(step == tile_cols)
    def _():
        for r in range(tile_rows):
            for ch in range(channels):
                rows = slice((r * channels + ch) * length, (r * channels + ch + 1) * length)
                lane = (r * channels + ch) * side
                put_rows(back, carry[rows, :], length, slice(lane, lane + side))

    @pl.when(step < blocks)
    def _():
        rays = dot(rows_out[...], back[...])
        for ch in range(channels):
            for r in range(tile_rows + 1):
                total = None
                if r < tile_rows:
                    lane = (r * channels + ch) * side
                    total = rays[0:side, lane : lane + side]
                if r > 0:
                    lane = ((r - 1) * channels + ch) * side
                    tail = rays[side:length, lane : lane + side]
                    total = tail if total is None else total + tail
                light[step, ch, r * side : (r + 1) * side, :] = total
        start_pair(light_down(step), light_up(step))

    @pl.when(jnp.logical_and(step >= 1, step < blocks + 1))
    def _():
        b = step - 1
        wait_pair(light_down(b), light_up(b))
        for ch in range(channels):
            for h in range(high_count):
                for o in range(low_count):
                    start = (h * low_count + o) * slab
                    value = light[b, ch, margin + start : margin + start + slab, :]
                    if start < margin:
                        value = value + light_above[b, ch, start : start + slab, :]
                    if start >= strip - margin:
                        start = start - (strip - margin)
                        value = value + light_below[b, ch, start : start + slab, :]
                    middle[b, o, h, ch] = value
        for d in range(1, low_count):
            to_low(b, d).start()

    @pl.when(jnp.logical_and(step >= 2, step < blocks + 2))
    def _():
        b = step - 2
        for d in range(1, low_count):
            to_low(b, d).wait()
        total = middle[b, low]
        for d in range(1, low_count):
            total = total + got_low[b, d - 1]
        part[b] = total
        for d in range(1, high_count):
            to_high(b, d).start()

    @pl.when(step >= 3)
    def _():
        b = step - 3
        for d in range(1, high_count):
            to_high(b, d).wait()
        total = part[b, high]
        for d in range(1, high_count):
            total = total + got_high[b, d - 1]
        out_ref[b] = total


def camera(scene, bank, weights, response, tile_count, wave_count):
    waves, tile_rows, tile_cols, side = bank.shape[:4]
    channels = response.shape[0]
    length, strip, margin = 2 * side, tile_rows * side, side // 2
    blocks = tile_cols + 1
    low_count = 1 << ((wave_count.bit_length() - 1) // 2)
    high_count = wave_count // low_count
    slab = strip // wave_count
    factors = tables(side)
    dims = (tile_count, low_count, high_count, tile_rows, tile_cols, side, waves, channels)
    smem = pl.BlockSpec(memory_space=pltpu.SMEM)
    vmem = pl.BlockSpec(memory_space=pltpu.VMEM)
    f32, bf16, sems = jnp.float32, jnp.bfloat16, pltpu.SemaphoreType.DMA
    tiles = tile_rows * waves
    planes = tile_rows * channels
    return pl.pallas_call(
        functools.partial(camera_kernel, dims),
        grid=(blocks + 3,),
        in_specs=[
            smem,
            smem,
            vmem,
            vmem,
            vmem,
            vmem,
            pl.BlockSpec((waves, strip, side), lambda s: (0, 0, jnp.minimum(s, tile_cols - 1))),
            vmem,
        ],
        out_specs=vmem,
        out_shape=jax.ShapeDtypeStruct((blocks, channels, slab, side), f32),
        scratch_shapes=[
            pltpu.VMEM((tile_cols, waves, side, side), f32),
            pltpu.VMEM((tile_cols, waves, side, side), f32),
            pltpu.VMEM((planes * length, side), f32),
            pltpu.VMEM((3 * side, tiles * side), bf16),
            pltpu.VMEM((tiles * length, 3 * side), bf16),
            pltpu.VMEM((tiles * length, length), f32),
            pltpu.VMEM((tiles * length, length), f32),
            pltpu.VMEM((planes * length, 3 * length), bf16),
            pltpu.VMEM((3 * length, planes * side), bf16),
            pltpu.VMEM((blocks, channels, strip + side, side), f32),
            pltpu.VMEM((blocks, channels, margin, side), f32),
            pltpu.VMEM((blocks, channels, margin, side), f32),
            pltpu.VMEM((blocks, low_count, high_count, channels, slab, side), f32),
            pltpu.VMEM((blocks, low_count - 1, high_count, channels, slab, side), f32),
            pltpu.VMEM((blocks, high_count, channels, slab, side), f32),
            pltpu.VMEM((blocks, high_count - 1, channels, slab, side), f32),
            sems((2, tile_cols)),
            sems((2, tile_cols)),
            sems((2, blocks)),
            sems((2, blocks)),
            sems((blocks, low_count - 1)),
            sems((blocks, low_count - 1)),
            sems((blocks, high_count - 1)),
            sems((blocks, high_count - 1)),
        ],
        compiler_params=pltpu.CompilerParams(
            vmem_limit_bytes=VMEM_BYTES, collective_id=0, has_side_effects=True
        ),
        cost_estimate=pl.CostEstimate(
            flops=tile_cols * (tiles * 24 + planes * 36) * 2 * side**3,
            bytes_accessed=8 * waves * strip * tile_cols * side,
            transcendentals=0,
        ),
        name="camera",
    )(weights, response, *factors, scene, bank)


def per_device(scene, bank, psf_index, psf_weight, response):
    waves, tile_rows, tile_cols, side = bank.shape[:4]
    margin = side // 2
    row_ids = lax.axis_index("tile") * tile_rows + lax.iota(jnp.int32, tile_rows)[:, None, None]
    col_ids = lax.iota(jnp.int32, tile_cols)[None, :, None]
    near = 3 * (psf_index // tile_cols - row_ids + 1) + psf_index % tile_cols - col_ids + 1
    fraction = psf_weight.astype(jnp.float32) / 65536.0
    weights = jnp.sum(jnp.where(near[..., None] == lax.iota(jnp.int32, 9), fraction[..., None], 0.0), axis=2)
    own_response = lax.dynamic_slice_in_dim(response, lax.axis_index("wave") * waves, waves, 1)
    blocks = camera(
        scene, bank, weights.reshape(-1), own_response, lax.axis_size("tile"), lax.axis_size("wave")
    )
    colour = blocks.transpose(1, 2, 0, 3).reshape(blocks.shape[1], blocks.shape[2], -1)
    return colour[:, :, margin : margin + tile_cols * side]


def solution(mesh):
    in_specs = (
        P("wave", "tile", None),
        P("wave", "tile", None, None, None),
        P("tile", None, None),
        P("tile", None, None),
        P(),
    )
    out_specs = P(None, ("tile", "wave"), None)
    return jax.shard_map(
        per_device, mesh=mesh, in_specs=in_specs, out_specs=out_specs, check_vma=False
    )
```

```python
import functools

import jax
import jax.numpy as jnp
import ml_dtypes
import numpy as np
from jax import lax
from jax.experimental import pallas as pl
from jax.experimental.pallas import tpu as pltpu
from jax.sharding import PartitionSpec as P

CHUNK_ROWS = 16
VMEM_BYTES = 56 * 1024 * 1024


def halves(table):
    high = table.astype(ml_dtypes.bfloat16)
    low = (table - high.astype(np.float64)).astype(ml_dtypes.bfloat16)
    return high, low


def left_factor(table):
    high, low = halves(table)
    return np.concatenate([high, high, low], axis=1)


def right_factor(table):
    high, low = halves(table)
    return np.concatenate([high, high, low], axis=0)


def tables(side):
    length = 2 * side
    odd = 2 * np.arange(side)[:, None] + 1
    angle = np.pi * (odd * np.arange(length)[None, :] % (2 * length)) / length
    cosine, sine = np.cos(angle), np.sin(angle)
    rows_in = np.concatenate([cosine[:, :side], -sine[:, :side]], axis=0)
    cols_in = np.concatenate([cosine[:, :side].T, sine[:, :side].T], axis=1)
    cols_out = np.concatenate([cosine, sine], axis=0)
    rows_out = np.concatenate([cosine.T, -sine.T], axis=1) * (2.0 / (length * length))
    return left_factor(rows_in), right_factor(cols_in), right_factor(cols_out), left_factor(rows_out)


def split(values):
    high = values.astype(jnp.bfloat16)
    low = (values - high.astype(jnp.float32)).astype(jnp.bfloat16)
    return high, low


def dot(left, right):
    return jnp.dot(left, right, preferred_element_type=jnp.float32)


def put_rows(out_ref, values, side, lanes):
    high, low = split(values)
    out_ref[0:side, lanes] = high
    out_ref[side : 2 * side, lanes] = low
    out_ref[2 * side : 3 * side, lanes] = high


def lift(values):
    high, low = split(values)
    return [high, low, high]


def camera_kernel(
    dims,
    index_ref,
    weight_ref,
    response_ref,
    rows_in,
    cols_in,
    cols_out,
    rows_out,
    scene_ref,
    bank_ref,
    out_ref,
    above,
    below,
    carry,
    scene_spec,
    psf_spec,
    mixed,
    back,
    light,
    light_above,
    light_below,
    middle,
    got_low,
    part,
    got_high,
    bank_sent,
    bank_got,
    light_sent,
    light_got,
    low_sent,
    low_got,
    high_sent,
    high_got,
):
    tile_count, low_count, high_count, tile_rows, tile_cols, entries, side, waves, channels = dims
    step = pl.program_id(0)
    length, margin, strip = 2 * side, side // 2, tile_rows * side
    slab = strip // (low_count * high_count)
    blocks = tile_cols + 1
    tile, wave = lax.axis_index("tile"), lax.axis_index("wave")
    low, high = lax.rem(wave, low_count), lax.div(wave, low_count)
    has_above, has_below = tile > 0, tile < tile_count - 1
    tile_above = lax.rem(tile + tile_count - 1, tile_count)
    tile_below = lax.rem(tile + 1, tile_count)

    def remote(src, dst, sent, got, axis, index):
        return pltpu.make_async_remote_copy(
            src_ref=src,
            dst_ref=dst,
            send_sem=sent,
            recv_sem=got,
            device_id={axis: index},
            device_id_type=pl.DeviceIdType.MESH,
        )

    def bank_down(c):
        return remote(
            bank_ref.at[:, tile_rows - 1, c], above.at[c], bank_sent.at[0, c], bank_got.at[0, c], "tile", tile_below
        )

    def bank_up(c):
        return remote(bank_ref.at[:, 0, c], below.at[c], bank_sent.at[1, c], bank_got.at[1, c], "tile", tile_above)

    def light_down(b):
        return remote(
            light.at[b, :, pl.ds(strip + margin, margin)],
            light_above.at[b],
            light_sent.at[0, b],
            light_got.at[0, b],
            "tile",
            tile_below,
        )

    def light_up(b):
        return remote(
            light.at[b, :, pl.ds(0, margin)], light_below.at[b], light_sent.at[1, b], light_got.at[1, b], "tile", tile_above
        )

    def start_pair(down, up):
        @pl.when(has_below)
        def _():
            down.start()

        @pl.when(has_above)
        def _():
            up.start()

    def wait_pair(down, up):
        @pl.when(has_below)
        def _():
            down.wait_send()
            up.wait_recv()

        @pl.when(has_above)
        def _():
            up.wait_send()
            down.wait_recv()

    def low_peer(d):
        return lax.rem(low + d, low_count)

    def high_peer(d):
        return lax.rem(high + d, high_count)

    def to_low(b, d):
        peer = low_peer(d)
        return remote(
            middle.at[b, peer],
            got_low.at[b, d - 1],
            low_sent.at[b, d - 1],
            low_got.at[b, d - 1],
            "wave",
            high * low_count + peer,
        )

    def to_high(b, d):
        peer = high_peer(d)
        return remote(
            part.at[b, peer],
            got_high.at[b, d - 1],
            high_sent.at[b, d - 1],
            high_got.at[b, d - 1],
            "wave",
            peer * low_count + low,
        )

    @pl.when(step == 0)
    def _():
        barrier = pltpu.get_barrier_semaphore()

        def greet(axis, index):
            pl.semaphore_signal(barrier, inc=1, device_id={axis: index}, device_id_type=pl.DeviceIdType.MESH)

        for d in range(1, low_count):
            greet("wave", high * low_count + low_peer(d))
        for d in range(1, high_count):
            greet("wave", high_peer(d) * low_count + low)

        @pl.when(has_above)
        def _():
            greet("tile", tile_above)

        @pl.when(has_below)
        def _():
            greet("tile", tile_below)

        others = low_count + high_count - 2
        pl.semaphore_wait(barrier, others + has_above.astype(jnp.int32) + has_below.astype(jnp.int32))
        for c in range(min(3, tile_cols)):
            start_pair(bank_down(c), bank_up(c))
        carry[...] = jnp.zeros_like(carry)

        @pl.when(jnp.logical_not(has_above))
        def _():
            above[...] = jnp.zeros_like(above)
            light_above[...] = jnp.zeros_like(light_above)

        @pl.when(jnp.logical_not(has_below))
        def _():
            below[...] = jnp.zeros_like(below)
            light_below[...] = jnp.zeros_like(light_below)

    @pl.when(jnp.logical_and(step > 0, step + 2 < tile_cols))
    def _():
        start_pair(bank_down(step + 2), bank_up(step + 2))

    def transform(spec, fields):
        tiles = tile_rows * waves
        for t in range(0, tiles, 2):
            pair = [jnp.concatenate(lift(field), axis=0) for field in (fields(t), fields(t + 1))]
            first = dot(rows_in[...], jnp.concatenate(pair, axis=1))
            pair = [jnp.concatenate(lift(first[:, j * side : (j + 1) * side]), axis=1) for j in range(2)]
            spec[t * length : (t + 2) * length, :] = dot(jnp.concatenate(pair, axis=0), cols_in[...])

    @pl.when(step < tile_cols)
    def _():
        def scene_field(t):
            r, w = divmod(t, waves)
            return scene_ref[w, r * side : (r + 1) * side, :]

        transform(scene_spec, scene_field)

        @pl.when(step == 0)
        def _():
            wait_pair(bank_down(0), bank_up(0))

        @pl.when(step + 1 < tile_cols)
        def _():
            wait_pair(bank_down(step + 1), bank_up(step + 1))

        near = (jnp.maximum(step - 1, 0), step, jnp.minimum(step + 1, tile_cols - 1))
        shares = []
        for r in range(tile_rows):
            here = (tile * tile_rows + r) * tile_cols + step
            listed = [(index_ref[r, k, step] - here, weight_ref[r, k, step]) for k in range(entries)]
            for i in range(3):
                for j in range(3):
                    offset = (i - 1) * tile_cols + j - 1
                    share = sum(jnp.where(away == offset, weight, 0) for away, weight in listed)
                    shares.append(share.astype(jnp.float32) * (1.0 / 65536.0))

        def psf_field(t):
            r, w = divmod(t, waves)
            psf = None
            for i in range(3):
                for j in range(3):
                    row = r + i - 1
                    if row < 0:
                        field = above[near[j], w]
                    elif row >= tile_rows:
                        field = below[near[j], w]
                    else:
                        field = bank_ref[w, row, near[j]]
                    term = shares[9 * r + 3 * i + j] * field
                    psf = term if psf is None else psf + term
            return psf

        transform(psf_spec, psf_field)

        def some_rows(r, index):
            start = index * CHUNK_ROWS
            left, right = slice(0, side), slice(side, length)
            sums = [None] * channels
            for w in range(waves):
                upper = pl.ds(start + (r * waves + w) * length, CHUNK_ROWS)
                lower = pl.ds(start + (r * waves + w) * length + side, CHUNK_ROWS)
                a, b, d, e = psf_spec[upper, left], psf_spec[upper, right], psf_spec[lower, left], psf_spec[lower, right]
                p1r, p1i, p2r, p2i = a + e, d - b, a - e, d + b
                a, b, d, e = (
                    scene_spec[upper, left],
                    scene_spec[upper, right],
                    scene_spec[lower, left],
                    scene_spec[lower, right],
                )
                s1r, s1i, s2r, s2i = a + e, d - b, a - e, d + b
                q1r, q1i = s1r * p1r - s1i * p1i, s1r * p1i + s1i * p1r
                q2r, q2i = s2r * p2r - s2i * p2i, s2r * p2i + s2i * p2r
                parts = (q1r + q2r, q2i - q1i, q1i + q2i, q1r - q2r)
                for ch in range(channels):
                    gain = response_ref[ch, wave * waves + w]
                    terms = [gain * value for value in parts]
                    sums[ch] = terms if w == 0 else [old + new for old, new in zip(sums[ch], terms)]
            for ch in range(channels):
                top = start + (r * channels + ch) * length
                for j, rows in ((0, pl.ds(top, CHUNK_ROWS)), (2, pl.ds(top + side, CHUNK_ROWS))):
                    for h in range(2):
                        upper_bits, lower_bits = split(sums[ch][j + h])
                        mixed[rows, h * side : (h + 1) * side] = upper_bits
                        mixed[rows, length + h * side : length + (h + 1) * side] = lower_bits
                        mixed[rows, 2 * length + h * side : 2 * length + (h + 1) * side] = upper_bits

        for r in range(tile_rows):
            for index in range(side // CHUNK_ROWS):
                some_rows(r, index)
        partial = dot(mixed[...], cols_out[...])
        for r in range(tile_rows):
            for ch in range(channels):
                rows = slice((r * channels + ch) * length, (r * channels + ch + 1) * length)
                lane = (r * channels + ch) * side
                put_rows(back, partial[rows, 0:side] + carry[rows, :], length, slice(lane, lane + side))
                carry[rows, :] = partial[rows, side:length]

    @pl.when(step == tile_cols)
    def _():
        for r in range(tile_rows):
            for ch in range(channels):
                rows = slice((r * channels + ch) * length, (r * channels + ch + 1) * length)
                lane = (r * channels + ch) * side
                put_rows(back, carry[rows, :], length, slice(lane, lane + side))

    @pl.when(step < blocks)
    def _():
        rays = dot(rows_out[...], back[...])
        for ch in range(channels):
            for r in range(tile_rows + 1):
                total = None
                if r < tile_rows:
                    lane = (r * channels + ch) * side
                    total = rays[0:side, lane : lane + side]
                if r > 0:
                    lane = ((r - 1) * channels + ch) * side
                    tail = rays[side:length, lane : lane + side]
                    total = tail if total is None else total + tail
                light[step, ch, r * side : (r + 1) * side, :] = total
        start_pair(light_down(step), light_up(step))

    @pl.when(jnp.logical_and(step >= 1, step < blocks + 1))
    def _():
        b = step - 1
        wait_pair(light_down(b), light_up(b))
        for ch in range(channels):
            for h in range(high_count):
                for o in range(low_count):
                    start = (h * low_count + o) * slab
                    value = light[b, ch, margin + start : margin + start + slab, :]
                    if start < margin:
                        value = value + light_above[b, ch, start : start + slab, :]
                    if start >= strip - margin:
                        start = start - (strip - margin)
                        value = value + light_below[b, ch, start : start + slab, :]
                    middle[b, o, h, ch] = value
        for d in range(1, low_count):
            to_low(b, d).start()

    @pl.when(jnp.logical_and(step >= 2, step < blocks + 2))
    def _():
        b = step - 2
        for d in range(1, low_count):
            to_low(b, d).wait()
        total = middle[b, low]
        for d in range(1, low_count):
            total = total + got_low[b, d - 1]
        part[b] = total
        for d in range(1, high_count):
            to_high(b, d).start()

    @pl.when(step >= 3)
    def _():
        b = step - 3
        for d in range(1, high_count):
            to_high(b, d).wait()
        total = part[b, high]
        for d in range(1, high_count):
            total = total + got_high[b, d - 1]
        out_ref[:, :, pl.ds(pl.multiple_of(b * side, side), side)] = total


def camera(scene, bank, index, weights, response, tile_count, wave_count):
    waves, tile_rows, tile_cols, side = bank.shape[:4]
    channels = response.shape[0]
    length, strip, margin = 2 * side, tile_rows * side, side // 2
    entries = index.shape[1]
    blocks = tile_cols + 1
    low_count = 1 << ((wave_count.bit_length() - 1) // 2)
    high_count = wave_count // low_count
    slab = strip // wave_count
    factors = tables(side)
    dims = (tile_count, low_count, high_count, tile_rows, tile_cols, entries, side, waves, channels)
    smem = pl.BlockSpec(memory_space=pltpu.SMEM)
    vmem = pl.BlockSpec(memory_space=pltpu.VMEM)
    f32, bf16, sems = jnp.float32, jnp.bfloat16, pltpu.SemaphoreType.DMA
    tiles = tile_rows * waves
    planes = tile_rows * channels
    return pl.pallas_call(
        functools.partial(camera_kernel, dims),
        grid=(blocks + 3,),
        in_specs=[
            smem,
            smem,
            smem,
            vmem,
            vmem,
            vmem,
            vmem,
            pl.BlockSpec((waves, strip, side), lambda s: (0, 0, jnp.minimum(s, tile_cols - 1))),
            vmem,
        ],
        out_specs=vmem,
        out_shape=jax.ShapeDtypeStruct((channels, slab, blocks * side), f32),
        scratch_shapes=[
            pltpu.VMEM((tile_cols, waves, side, side), f32),
            pltpu.VMEM((tile_cols, waves, side, side), f32),
            pltpu.VMEM((planes * length, side), f32),
            pltpu.VMEM((tiles * length, length), f32),
            pltpu.VMEM((tiles * length, length), f32),
            pltpu.VMEM((planes * length, 3 * length), bf16),
            pltpu.VMEM((3 * length, planes * side), bf16),
            pltpu.VMEM((blocks, channels, strip + side, side), f32),
            pltpu.VMEM((blocks, channels, margin, side), f32),
            pltpu.VMEM((blocks, channels, margin, side), f32),
            pltpu.VMEM((blocks, low_count, high_count, channels, slab, side), f32),
            pltpu.VMEM((blocks, low_count - 1, high_count, channels, slab, side), f32),
            pltpu.VMEM((blocks, high_count, channels, slab, side), f32),
            pltpu.VMEM((blocks, high_count - 1, channels, slab, side), f32),
            sems((2, tile_cols)),
            sems((2, tile_cols)),
            sems((2, blocks)),
            sems((2, blocks)),
            sems((blocks, low_count - 1)),
            sems((blocks, low_count - 1)),
            sems((blocks, high_count - 1)),
            sems((blocks, high_count - 1)),
        ],
        compiler_params=pltpu.CompilerParams(
            vmem_limit_bytes=VMEM_BYTES, collective_id=0, has_side_effects=True
        ),
        cost_estimate=pl.CostEstimate(
            flops=tile_cols * (tiles * 24 + planes * 36) * 2 * side**3,
            bytes_accessed=8 * waves * strip * tile_cols * side,
            transcendentals=0,
        ),
        name="camera",
    )(index, weights, response, *factors, scene, bank)


def per_device(scene, bank, psf_index, psf_weight, response):
    tile_cols, side = bank.shape[2:4]
    margin = side // 2
    colour = camera(
        scene,
        bank,
        psf_index.transpose(0, 2, 1),
        psf_weight.transpose(0, 2, 1),
        response,
        lax.axis_size("tile"),
        lax.axis_size("wave"),
    )
    return colour[:, :, margin : margin + tile_cols * side]


def solution(mesh):
    in_specs = (
        P("wave", "tile", None),
        P("wave", "tile", None, None, None),
        P("tile", None, None),
        P("tile", None, None),
        P(),
    )
    out_specs = P(None, ("tile", "wave"), None)
    return jax.shard_map(
        per_device, mesh=mesh, in_specs=in_specs, out_specs=out_specs, check_vma=False
    )
```

```python
import functools

import jax
import jax.numpy as jnp
import ml_dtypes
import numpy as np
from jax import lax
from jax.experimental import pallas as pl
from jax.experimental.pallas import tpu as pltpu
from jax.sharding import PartitionSpec as P

CHUNK_ROWS = 16
VMEM_BYTES = 56 * 1024 * 1024


def halves(table):
    high = table.astype(ml_dtypes.bfloat16)
    low = (table - high.astype(np.float64)).astype(ml_dtypes.bfloat16)
    return high, low


def left_factor(table):
    high, low = halves(table)
    return np.concatenate([high, high, low], axis=1)


def right_factor(table):
    high, low = halves(table)
    return np.concatenate([high, high, low], axis=0)


def tables(side):
    length = 2 * side
    odd = 2 * np.arange(side)[:, None] + 1
    angle = np.pi * (odd * np.arange(length)[None, :] % (2 * length)) / length
    cosine, sine = np.cos(angle), np.sin(angle)
    rows_in = np.concatenate([cosine[:, :side], -sine[:, :side]], axis=0)
    cols_in = np.concatenate([cosine[:, :side].T, sine[:, :side].T], axis=1)
    cols_out = np.concatenate([cosine, sine], axis=0)
    rows_out = np.concatenate([cosine.T, -sine.T], axis=1) * (2.0 / (length * length))
    return left_factor(rows_in), right_factor(cols_in), right_factor(cols_out), left_factor(rows_out)


def split(values):
    high = values.astype(jnp.bfloat16)
    low = (values - high.astype(jnp.float32)).astype(jnp.bfloat16)
    return high, low


def dot(left, right):
    return jnp.dot(left, right, preferred_element_type=jnp.float32)


def put_rows(out_ref, values, side, lanes):
    high, low = split(values)
    out_ref[0:side, lanes] = high
    out_ref[side : 2 * side, lanes] = low
    out_ref[2 * side : 3 * side, lanes] = high


def lift(values):
    high, low = split(values)
    return [high, low, high]


def camera_kernel(
    dims,
    index_ref,
    weight_ref,
    response_ref,
    rows_in,
    cols_in,
    cols_out,
    rows_out,
    scene_ref,
    bank_ref,
    out_ref,
    above,
    below,
    carry,
    scene_next,
    scene_spec,
    psf_spec,
    mixed,
    back,
    last,
    light,
    light_above,
    light_below,
    middle,
    got_low,
    part,
    got_high,
    bank_sent,
    bank_got,
    light_sent,
    light_got,
    low_sent,
    low_got,
    high_sent,
    high_got,
):
    tile_count, low_count, high_count, tile_rows, tile_cols, entries, side, waves, channels = dims
    step = pl.program_id(0)
    length, margin, strip = 2 * side, side // 2, tile_rows * side
    slab = strip // (low_count * high_count)
    blocks = tile_cols + 1
    tile, wave = lax.axis_index("tile"), lax.axis_index("wave")
    low, high = lax.rem(wave, low_count), lax.div(wave, low_count)
    has_above, has_below = tile > 0, tile < tile_count - 1
    tile_above = lax.rem(tile + tile_count - 1, tile_count)
    tile_below = lax.rem(tile + 1, tile_count)

    def remote(src, dst, sent, got, axis, index):
        return pltpu.make_async_remote_copy(
            src_ref=src,
            dst_ref=dst,
            send_sem=sent,
            recv_sem=got,
            device_id={axis: index},
            device_id_type=pl.DeviceIdType.MESH,
        )

    def bank_down(c):
        return remote(
            bank_ref.at[:, tile_rows - 1, c], above.at[c], bank_sent.at[0, c], bank_got.at[0, c], "tile", tile_below
        )

    def bank_up(c):
        return remote(bank_ref.at[:, 0, c], below.at[c], bank_sent.at[1, c], bank_got.at[1, c], "tile", tile_above)

    def light_down(b):
        return remote(
            light.at[b, :, pl.ds(strip + margin, margin)],
            light_above.at[b],
            light_sent.at[0, b],
            light_got.at[0, b],
            "tile",
            tile_below,
        )

    def light_up(b):
        return remote(
            light.at[b, :, pl.ds(0, margin)], light_below.at[b], light_sent.at[1, b], light_got.at[1, b], "tile", tile_above
        )

    def start_pair(down, up):
        @pl.when(has_below)
        def _():
            down.start()

        @pl.when(has_above)
        def _():
            up.start()

    def wait_pair(down, up):
        @pl.when(has_below)
        def _():
            down.wait_send()
            up.wait_recv()

        @pl.when(has_above)
        def _():
            up.wait_send()
            down.wait_recv()

    def low_peer(d):
        return lax.rem(low + d, low_count)

    def high_peer(d):
        return lax.rem(high + d, high_count)

    def to_low(b, d):
        peer = low_peer(d)
        return remote(
            middle.at[b, peer],
            got_low.at[b, d - 1],
            low_sent.at[b, d - 1],
            low_got.at[b, d - 1],
            "wave",
            high * low_count + peer,
        )

    def to_high(b, d):
        peer = high_peer(d)
        return remote(
            part.at[b, peer],
            got_high.at[b, d - 1],
            high_sent.at[b, d - 1],
            high_got.at[b, d - 1],
            "wave",
            peer * low_count + low,
        )

    @pl.when(step == 0)
    def _():
        barrier = pltpu.get_barrier_semaphore()

        def greet(axis, index):
            pl.semaphore_signal(barrier, inc=1, device_id={axis: index}, device_id_type=pl.DeviceIdType.MESH)

        for d in range(1, low_count):
            greet("wave", high * low_count + low_peer(d))
        for d in range(1, high_count):
            greet("wave", high_peer(d) * low_count + low)

        @pl.when(has_above)
        def _():
            greet("tile", tile_above)

        @pl.when(has_below)
        def _():
            greet("tile", tile_below)

        others = low_count + high_count - 2
        pl.semaphore_wait(barrier, others + has_above.astype(jnp.int32) + has_below.astype(jnp.int32))
        for c in range(2):
            start_pair(bank_down(c), bank_up(c))
        carry[...] = jnp.zeros_like(carry)

        @pl.when(jnp.logical_not(has_above))
        def _():
            above[...] = jnp.zeros_like(above)
            light_above[...] = jnp.zeros_like(light_above)

        @pl.when(jnp.logical_not(has_below))
        def _():
            below[...] = jnp.zeros_like(below)
            light_below[...] = jnp.zeros_like(light_below)

    def transform(spec, fields, t):
        pair = [jnp.concatenate(lift(field), axis=0) for field in (fields(t), fields(t + 1))]
        first = dot(rows_in[...], jnp.concatenate(pair, axis=1))
        pair = [jnp.concatenate(lift(first[:, j * side : (j + 1) * side]), axis=1) for j in range(2)]
        spec[t * length : (t + 2) * length, :] = dot(jnp.concatenate(pair, axis=0), cols_in[...])

    def scene_field(t):
        r, w = divmod(t, waves)
        return scene_ref[w, r * side : (r + 1) * side, :]

    tiles = tile_rows * waves

    @pl.when(step == 0)
    def _():
        for t in range(0, tiles, 2):
            transform(scene_next, scene_field, t)

    @pl.when(step == 1)
    def _():
        wait_pair(bank_down(0), bank_up(0))

    @pl.when(jnp.logical_and(step >= 1, step < tile_cols))
    def _():
        wait_pair(bank_down(step), bank_up(step))

        @pl.when(step + 1 < tile_cols)
        def _():
            start_pair(bank_down(step + 1), bank_up(step + 1))

    @pl.when(jnp.logical_and(step >= 1, step <= tile_cols))
    def _():
        col = step - 1
        near = (jnp.maximum(col - 1, 0), col, jnp.minimum(col + 1, tile_cols - 1))
        shares = []
        for r in range(tile_rows):
            here = (tile * tile_rows + r) * tile_cols + col
            listed = [(index_ref[r, k, col] - here, weight_ref[r, k, col]) for k in range(entries)]
            for i in range(3):
                for j in range(3):
                    offset = (i - 1) * tile_cols + j - 1
                    share = sum(jnp.where(away == offset, weight, 0) for away, weight in listed)
                    shares.append(share.astype(jnp.float32) * (1.0 / 65536.0))

        def psf_field(t):
            r, w = divmod(t, waves)
            psf = None
            for i in range(3):
                for j in range(3):
                    row = r + i - 1
                    if row < 0:
                        field = above[near[j], w]
                    elif row >= tile_rows:
                        field = below[near[j], w]
                    else:
                        field = bank_ref[w, row, near[j]]
                    term = shares[9 * r + 3 * i + j] * field
                    psf = term if psf is None else psf + term
            return psf

        for t in range(tiles):
            top = t * length
            upper, lower = slice(top, top + side), slice(top + side, top + length)
            left, right = slice(0, side), slice(side, length)
            a, b, d, e = (
                scene_next[upper, left],
                scene_next[upper, right],
                scene_next[lower, left],
                scene_next[lower, right],
            )
            scene_spec[upper, left], scene_spec[lower, left] = a + e, d - b
            scene_spec[upper, right], scene_spec[lower, right] = a - e, d + b
            if t % 2 == 1:
                transform(psf_spec, psf_field, t - 1)

        def some_rows(r, index):
            start = index * CHUNK_ROWS
            left, right = slice(0, side), slice(side, length)
            sums = [None] * channels
            for w in range(waves):
                upper = pl.ds(start + (r * waves + w) * length, CHUNK_ROWS)
                lower = pl.ds(start + (r * waves + w) * length + side, CHUNK_ROWS)
                a, b, d, e = psf_spec[upper, left], psf_spec[upper, right], psf_spec[lower, left], psf_spec[lower, right]
                p1r, p1i, p2r, p2i = a + e, d - b, a - e, d + b
                s1r, s1i = scene_spec[upper, left], scene_spec[lower, left]
                s2r, s2i = scene_spec[upper, right], scene_spec[lower, right]
                q1r, q1i = s1r * p1r - s1i * p1i, s1r * p1i + s1i * p1r
                q2r, q2i = s2r * p2r - s2i * p2i, s2r * p2i + s2i * p2r
                parts = (q1r + q2r, q2i - q1i, q1i + q2i, q1r - q2r)
                for ch in range(channels):
                    gain = response_ref[ch, wave * waves + w]
                    terms = [gain * value for value in parts]
                    sums[ch] = terms if w == 0 else [old + new for old, new in zip(sums[ch], terms)]
            for ch in range(channels):
                top = start + (r * channels + ch) * length
                for j, rows in ((0, pl.ds(top, CHUNK_ROWS)), (2, pl.ds(top + side, CHUNK_ROWS))):
                    for h in range(2):
                        upper_bits, lower_bits = split(sums[ch][j + h])
                        mixed[rows, h * side : (h + 1) * side] = upper_bits
                        mixed[rows, length + h * side : length + (h + 1) * side] = lower_bits
                        mixed[rows, 2 * length + h * side : 2 * length + (h + 1) * side] = upper_bits

        ahead = list(range(0, tiles, 2))
        chunks = side // CHUNK_ROWS
        every = max(1, tile_rows * chunks // len(ahead))
        for r in range(tile_rows):
            for index in range(chunks):
                some_rows(r, index)
                if (r * chunks + index + 1) % every == every // 2 and ahead:
                    transform(scene_next, scene_field, ahead.pop(0))
            planes = slice(r * channels * length, (r + 1) * channels * length)
            partial = dot(mixed[planes, :], cols_out[...])
            for ch in range(channels):
                rows = slice((r * channels + ch) * length, (r * channels + ch + 1) * length)
                lane = (r * channels + ch) * side
                block = partial[ch * length : (ch + 1) * length, :]
                put_rows(back, block[:, 0:side] + carry[rows, :], length, slice(lane, lane + side))
                carry[rows, :] = block[:, side:length]

    @pl.when(step == tile_cols + 1)
    def _():
        for r in range(tile_rows):
            for ch in range(channels):
                rows = slice((r * channels + ch) * length, (r * channels + ch + 1) * length)
                lane = (r * channels + ch) * side
                put_rows(back, carry[rows, :], length, slice(lane, lane + side))

    @pl.when(jnp.logical_and(step >= 1, step <= blocks))
    def _():
        now = step - 1
        rays = dot(rows_out[...], back[...])
        for ch in range(channels):
            for r in range(tile_rows + 1):
                total = None
                if r < tile_rows:
                    lane = (r * channels + ch) * side
                    total = rays[0:side, lane : lane + side]
                if r > 0:
                    lane = ((r - 1) * channels + ch) * side
                    tail = rays[side:length, lane : lane + side]
                    total = tail if total is None else total + tail
                light[now, ch, r * side : (r + 1) * side, :] = total
        start_pair(light_down(now), light_up(now))

    @pl.when(jnp.logical_and(step >= 2, step < blocks + 2))
    def _():
        b = step - 2
        wait_pair(light_down(b), light_up(b))
        for ch in range(channels):
            for h in range(high_count):
                for o in range(low_count):
                    start = (h * low_count + o) * slab
                    value = light[b, ch, margin + start : margin + start + slab, :]
                    if start < margin:
                        value = value + light_above[b, ch, start : start + slab, :]
                    if start >= strip - margin:
                        start = start - (strip - margin)
                        value = value + light_below[b, ch, start : start + slab, :]
                    middle[b, o, h, ch] = value
        for d in range(1, low_count):
            to_low(b, d).start()

    @pl.when(jnp.logical_and(step >= 3, step < blocks + 3))
    def _():
        b = step - 3
        for d in range(1, low_count):
            to_low(b, d).wait()
        total = middle[b, low]
        for d in range(1, low_count):
            total = total + got_low[b, d - 1]
        part[b] = total
        for d in range(1, high_count):
            to_high(b, d).start()

    @pl.when(step >= 4)
    def _():
        b = step - 4
        for d in range(1, high_count):
            to_high(b, d).wait()
        total = part[b, high]
        for d in range(1, high_count):
            total = total + got_high[b, d - 1]
        turned = pltpu.roll(total.reshape(channels * slab, side), margin, 1)

        @pl.when(b > 0)
        def _():
            is_left = lax.broadcasted_iota(jnp.int32, turned.shape, 1) < margin
            whole = jnp.where(is_left, last[...], turned).reshape(channels, slab, side)
            out_ref[:, :, pl.ds(pl.multiple_of((b - 1) * side, side), side)] = whole

        last[...] = turned


def camera(scene, bank, index, weights, response, tile_count, wave_count):
    waves, tile_rows, tile_cols, side = bank.shape[:4]
    channels = response.shape[0]
    length, strip, margin = 2 * side, tile_rows * side, side // 2
    entries = index.shape[1]
    blocks = tile_cols + 1
    low_count = 1 << ((wave_count.bit_length() - 1) // 2)
    high_count = wave_count // low_count
    slab = strip // wave_count
    factors = tables(side)
    dims = (tile_count, low_count, high_count, tile_rows, tile_cols, entries, side, waves, channels)
    smem = pl.BlockSpec(memory_space=pltpu.SMEM)
    vmem = pl.BlockSpec(memory_space=pltpu.VMEM)
    f32, bf16, sems = jnp.float32, jnp.bfloat16, pltpu.SemaphoreType.DMA
    tiles = tile_rows * waves
    planes = tile_rows * channels
    return pl.pallas_call(
        functools.partial(camera_kernel, dims),
        grid=(blocks + 4,),
        in_specs=[
            smem,
            smem,
            smem,
            vmem,
            vmem,
            vmem,
            vmem,
            pl.BlockSpec((waves, strip, side), lambda s: (0, 0, jnp.minimum(s, tile_cols - 1))),
            vmem,
        ],
        out_specs=vmem,
        out_shape=jax.ShapeDtypeStruct((channels, slab, tile_cols * side), f32),
        scratch_shapes=[
            pltpu.VMEM((tile_cols, waves, side, side), f32),
            pltpu.VMEM((tile_cols, waves, side, side), f32),
            pltpu.VMEM((planes * length, side), f32),
            pltpu.VMEM((tiles * length, length), f32),
            pltpu.VMEM((tiles * length, length), f32),
            pltpu.VMEM((tiles * length, length), f32),
            pltpu.VMEM((planes * length, 3 * length), bf16),
            pltpu.VMEM((3 * length, planes * side), bf16),
            pltpu.VMEM((channels * slab, side), f32),
            pltpu.VMEM((blocks, channels, strip + side, side), f32),
            pltpu.VMEM((blocks, channels, margin, side), f32),
            pltpu.VMEM((blocks, channels, margin, side), f32),
            pltpu.VMEM((blocks, low_count, high_count, channels, slab, side), f32),
            pltpu.VMEM((blocks, low_count - 1, high_count, channels, slab, side), f32),
            pltpu.VMEM((blocks, high_count, channels, slab, side), f32),
            pltpu.VMEM((blocks, high_count - 1, channels, slab, side), f32),
            sems((2, tile_cols)),
            sems((2, tile_cols)),
            sems((2, blocks)),
            sems((2, blocks)),
            sems((blocks, low_count - 1)),
            sems((blocks, low_count - 1)),
            sems((blocks, high_count - 1)),
            sems((blocks, high_count - 1)),
        ],
        compiler_params=pltpu.CompilerParams(
            vmem_limit_bytes=VMEM_BYTES, collective_id=0, has_side_effects=True
        ),
        cost_estimate=pl.CostEstimate(
            flops=tile_cols * (tiles * 24 + planes * 36) * 2 * side**3,
            bytes_accessed=8 * waves * strip * tile_cols * side,
            transcendentals=0,
        ),
        name="camera",
    )(index, weights, response, *factors, scene, bank)


def per_device(scene, bank, psf_index, psf_weight, response):
    return camera(
        scene,
        bank,
        psf_index.transpose(0, 2, 1),
        psf_weight.transpose(0, 2, 1),
        response,
        lax.axis_size("tile"),
        lax.axis_size("wave"),
    )


def solution(mesh):
    in_specs = (
        P("wave", "tile", None),
        P("wave", "tile", None, None, None),
        P("tile", None, None),
        P("tile", None, None),
        P(),
    )
    out_specs = P(None, ("tile", "wave"), None)
    return jax.shard_map(
        per_device, mesh=mesh, in_specs=in_specs, out_specs=out_specs, check_vma=False
    )
```

```python
import functools

import jax
import jax.numpy as jnp
import ml_dtypes
import numpy as np
from jax import lax
from jax.experimental import pallas as pl
from jax.experimental.pallas import tpu as pltpu
from jax.sharding import PartitionSpec as P

CHUNK_ROWS = 16
VMEM_BYTES = 56 * 1024 * 1024


def halves(table):
    high = table.astype(ml_dtypes.bfloat16)
    low = (table - high.astype(np.float64)).astype(ml_dtypes.bfloat16)
    return high, low


def left_factor(table):
    high, low = halves(table)
    return np.concatenate([high, high, low], axis=1)


def right_factor(table):
    high, low = halves(table)
    return np.concatenate([high, high, low], axis=0)


def tables(side):
    length = 2 * side
    odd = 2 * np.arange(side)[:, None] + 1
    angle = np.pi * (odd * np.arange(length)[None, :] % (2 * length)) / length
    cosine, sine = np.cos(angle), np.sin(angle)
    rows_in = np.concatenate([cosine[:, :side], -sine[:, :side]], axis=0)
    cols_in = np.concatenate([cosine[:, :side].T, sine[:, :side].T], axis=1)
    cols_out = np.concatenate([cosine, sine], axis=0)
    rows_out = np.concatenate([cosine.T, -sine.T], axis=1) * (2.0 / (length * length))
    return left_factor(rows_in), right_factor(cols_in), right_factor(cols_out), left_factor(rows_out)


def split(values):
    high = values.astype(jnp.bfloat16)
    low = (values - high.astype(jnp.float32)).astype(jnp.bfloat16)
    return high, low


def dot(left, right):
    return jnp.dot(left, right, preferred_element_type=jnp.float32)


def put_rows(out_ref, values, side, lanes):
    high, low = split(values)
    out_ref[0:side, lanes] = high
    out_ref[side : 2 * side, lanes] = low
    out_ref[2 * side : 3 * side, lanes] = high


def lift(values):
    high, low = split(values)
    return [high, low, high]


def camera_kernel(
    dims,
    index_ref,
    weight_ref,
    response_ref,
    rows_in,
    cols_in,
    cols_out,
    rows_out,
    scene_ref,
    bank_ref,
    out_ref,
    above,
    below,
    carry,
    scene_mid,
    psf_mid,
    mixed,
    back,
    last,
    light,
    light_above,
    light_below,
    middle,
    got_low,
    part,
    got_high,
    bank_sent,
    bank_got,
    light_sent,
    light_got,
    low_sent,
    low_got,
    high_sent,
    high_got,
):
    tile_count, low_count, high_count, tile_rows, tile_cols, entries, side, waves, channels = dims
    step = pl.program_id(0)
    length, margin, strip = 2 * side, side // 2, tile_rows * side
    slab = strip // (low_count * high_count)
    blocks = tile_cols + 1
    tile, wave = lax.axis_index("tile"), lax.axis_index("wave")
    low, high = lax.rem(wave, low_count), lax.div(wave, low_count)
    has_above, has_below = tile > 0, tile < tile_count - 1
    tile_above = lax.rem(tile + tile_count - 1, tile_count)
    tile_below = lax.rem(tile + 1, tile_count)

    def remote(src, dst, sent, got, axis, index):
        return pltpu.make_async_remote_copy(
            src_ref=src,
            dst_ref=dst,
            send_sem=sent,
            recv_sem=got,
            device_id={axis: index},
            device_id_type=pl.DeviceIdType.MESH,
        )

    def bank_down(c):
        return remote(
            bank_ref.at[:, tile_rows - 1, c], above.at[c], bank_sent.at[0, c], bank_got.at[0, c], "tile", tile_below
        )

    def bank_up(c):
        return remote(bank_ref.at[:, 0, c], below.at[c], bank_sent.at[1, c], bank_got.at[1, c], "tile", tile_above)

    def light_down(b):
        return remote(
            light.at[b, :, pl.ds(strip + margin, margin)],
            light_above.at[b],
            light_sent.at[0, b],
            light_got.at[0, b],
            "tile",
            tile_below,
        )

    def light_up(b):
        return remote(
            light.at[b, :, pl.ds(0, margin)], light_below.at[b], light_sent.at[1, b], light_got.at[1, b], "tile", tile_above
        )

    def start_pair(down, up):
        @pl.when(has_below)
        def _():
            down.start()

        @pl.when(has_above)
        def _():
            up.start()

    def wait_pair(down, up):
        @pl.when(has_below)
        def _():
            down.wait_send()
            up.wait_recv()

        @pl.when(has_above)
        def _():
            up.wait_send()
            down.wait_recv()

    def low_peer(d):
        return lax.rem(low + d, low_count)

    def high_peer(d):
        return lax.rem(high + d, high_count)

    def to_low(b, d):
        peer = low_peer(d)
        return remote(
            middle.at[b, peer],
            got_low.at[b, d - 1],
            low_sent.at[b, d - 1],
            low_got.at[b, d - 1],
            "wave",
            high * low_count + peer,
        )

    def to_high(b, d):
        peer = high_peer(d)
        return remote(
            part.at[b, peer],
            got_high.at[b, d - 1],
            high_sent.at[b, d - 1],
            high_got.at[b, d - 1],
            "wave",
            peer * low_count + low,
        )

    @pl.when(step == 0)
    def _():
        barrier = pltpu.get_barrier_semaphore()

        def greet(axis, index):
            pl.semaphore_signal(barrier, inc=1, device_id={axis: index}, device_id_type=pl.DeviceIdType.MESH)

        for d in range(1, low_count):
            greet("wave", high * low_count + low_peer(d))
        for d in range(1, high_count):
            greet("wave", high_peer(d) * low_count + low)

        @pl.when(has_above)
        def _():
            greet("tile", tile_above)

        @pl.when(has_below)
        def _():
            greet("tile", tile_below)

        others = low_count + high_count - 2
        pl.semaphore_wait(barrier, others + has_above.astype(jnp.int32) + has_below.astype(jnp.int32))
        for c in range(2):
            start_pair(bank_down(c), bank_up(c))
        carry[...] = jnp.zeros_like(carry)

        @pl.when(jnp.logical_not(has_above))
        def _():
            above[...] = jnp.zeros_like(above)
            light_above[...] = jnp.zeros_like(light_above)

        @pl.when(jnp.logical_not(has_below))
        def _():
            below[...] = jnp.zeros_like(below)
            light_below[...] = jnp.zeros_like(light_below)

    def transform_rows(mid, fields, t):
        pair = [jnp.concatenate(lift(field), axis=0) for field in (fields(t), fields(t + 1))]
        first = dot(rows_in[...], jnp.concatenate(pair, axis=1))
        for j in range(2):
            upper_bits, lower_bits = split(first[:, j * side : (j + 1) * side])
            rows = slice((t + j) * length, (t + j + 1) * length)
            mid[rows, 0:side] = upper_bits
            mid[rows, side:length] = lower_bits

    def scene_field(t):
        r, w = divmod(t, waves)
        return scene_ref[w, r * side : (r + 1) * side, :]

    tiles = tile_rows * waves

    @pl.when(step < tile_cols)
    def _():
        col = step
        for t in range(0, tiles, 2):
            transform_rows(scene_mid, scene_field, t)

        @pl.when(step == 0)
        def _():
            wait_pair(bank_down(0), bank_up(0))

        @pl.when(step + 1 < tile_cols)
        def _():
            wait_pair(bank_down(step + 1), bank_up(step + 1))

        @pl.when(step + 2 < tile_cols)
        def _():
            start_pair(bank_down(step + 2), bank_up(step + 2))

        near = (jnp.maximum(col - 1, 0), col, jnp.minimum(col + 1, tile_cols - 1))
        shares = []
        for r in range(tile_rows):
            here = (tile * tile_rows + r) * tile_cols + col
            listed = [(index_ref[r, k, col] - here, weight_ref[r, k, col]) for k in range(entries)]
            for i in range(3):
                for j in range(3):
                    offset = (i - 1) * tile_cols + j - 1
                    share = sum(jnp.where(away == offset, weight, 0) for away, weight in listed)
                    shares.append(share.astype(jnp.float32) * (1.0 / 65536.0))

        def psf_field(t):
            r, w = divmod(t, waves)
            psf = None
            for i in range(3):
                for j in range(3):
                    row = r + i - 1
                    if row < 0:
                        field = above[near[j], w]
                    elif row >= tile_rows:
                        field = below[near[j], w]
                    else:
                        field = bank_ref[w, row, near[j]]
                    term = shares[9 * r + 3 * i + j] * field
                    psf = term if psf is None else psf + term
            return psf

        for t in range(0, tiles, 2):
            transform_rows(psf_mid, psf_field, t)

        def some_rows(r, index):
            start = index * CHUNK_ROWS
            lines = []
            for w in range(waves):
                top = start + (r * waves + w) * length
                for mid in (scene_mid, psf_mid):
                    for first in (top, top + side):
                        both = mid[first : first + CHUNK_ROWS, :]
                        lines.append(jnp.concatenate([both, both[:, 0:side]], axis=1))
            spec = dot(jnp.concatenate(lines, axis=0), cols_in[...])

            def quarters(block):
                top = block * 2 * CHUNK_ROWS
                upper, lower = slice(top, top + CHUNK_ROWS), slice(top + CHUNK_ROWS, top + 2 * CHUNK_ROWS)
                a, b, d, e = spec[upper, :side], spec[upper, side:], spec[lower, :side], spec[lower, side:]
                return a + e, d - b, a - e, d + b

            sums = [None] * channels
            for w in range(waves):
                s1r, s1i, s2r, s2i = quarters(2 * w)
                p1r, p1i, p2r, p2i = quarters(2 * w + 1)
                q1r, q1i = s1r * p1r - s1i * p1i, s1r * p1i + s1i * p1r
                q2r, q2i = s2r * p2r - s2i * p2i, s2r * p2i + s2i * p2r
                parts = (q1r + q2r, q2i - q1i, q1i + q2i, q1r - q2r)
                for ch in range(channels):
                    gain = response_ref[ch, wave * waves + w]
                    terms = [gain * value for value in parts]
                    sums[ch] = terms if w == 0 else [old + new for old, new in zip(sums[ch], terms)]
            for ch in range(channels):
                top = start + (r * channels + ch) * length
                for j, rows in ((0, pl.ds(top, CHUNK_ROWS)), (2, pl.ds(top + side, CHUNK_ROWS))):
                    for h in range(2):
                        upper_bits, lower_bits = split(sums[ch][j + h])
                        mixed[rows, h * side : (h + 1) * side] = upper_bits
                        mixed[rows, length + h * side : length + (h + 1) * side] = lower_bits
                        mixed[rows, 2 * length + h * side : 2 * length + (h + 1) * side] = upper_bits

        for r in range(tile_rows):
            for index in range(side // CHUNK_ROWS):
                some_rows(r, index)
            planes = slice(r * channels * length, (r + 1) * channels * length)
            partial = dot(mixed[planes, :], cols_out[...])
            for ch in range(channels):
                rows = slice((r * channels + ch) * length, (r * channels + ch + 1) * length)
                lane = (r * channels + ch) * side
                block = partial[ch * length : (ch + 1) * length, :]
                put_rows(back, block[:, 0:side] + carry[rows, :], length, slice(lane, lane + side))
                carry[rows, :] = block[:, side:length]

    @pl.when(step == tile_cols)
    def _():
        for r in range(tile_rows):
            for ch in range(channels):
                rows = slice((r * channels + ch) * length, (r * channels + ch + 1) * length)
                lane = (r * channels + ch) * side
                put_rows(back, carry[rows, :], length, slice(lane, lane + side))

    @pl.when(step < blocks)
    def _():
        now = step
        rays = dot(rows_out[...], back[...])
        for ch in range(channels):
            for r in range(tile_rows + 1):
                total = None
                if r < tile_rows:
                    lane = (r * channels + ch) * side
                    total = rays[0:side, lane : lane + side]
                if r > 0:
                    lane = ((r - 1) * channels + ch) * side
                    tail = rays[side:length, lane : lane + side]
                    total = tail if total is None else total + tail
                light[now, ch, r * side : (r + 1) * side, :] = total
        start_pair(light_down(now), light_up(now))

    @pl.when(jnp.logical_and(step >= 1, step < blocks + 1))
    def _():
        b = step - 1
        wait_pair(light_down(b), light_up(b))
        for ch in range(channels):
            for h in range(high_count):
                for o in range(low_count):
                    start = (h * low_count + o) * slab
                    value = light[b, ch, margin + start : margin + start + slab, :]
                    if start < margin:
                        value = value + light_above[b, ch, start : start + slab, :]
                    if start >= strip - margin:
                        start = start - (strip - margin)
                        value = value + light_below[b, ch, start : start + slab, :]
                    middle[b, o, h, ch] = value
        for d in range(1, low_count):
            to_low(b, d).start()

    @pl.when(jnp.logical_and(step >= 2, step < blocks + 2))
    def _():
        b = step - 2
        for d in range(1, low_count):
            to_low(b, d).wait()
        total = middle[b, low]
        for d in range(1, low_count):
            total = total + got_low[b, d - 1]
        part[b] = total
        for d in range(1, high_count):
            to_high(b, d).start()

    @pl.when(step >= 3)
    def _():
        b = step - 3
        for d in range(1, high_count):
            to_high(b, d).wait()
        total = part[b, high]
        for d in range(1, high_count):
            total = total + got_high[b, d - 1]
        turned = pltpu.roll(total.reshape(channels * slab, side), margin, 1)

        @pl.when(b > 0)
        def _():
            is_left = lax.broadcasted_iota(jnp.int32, turned.shape, 1) < margin
            whole = jnp.where(is_left, last[...], turned).reshape(channels, slab, side)
            out_ref[:, :, pl.ds(pl.multiple_of((b - 1) * side, side), side)] = whole

        last[...] = turned


def camera(scene, bank, index, weights, response, tile_count, wave_count):
    waves, tile_rows, tile_cols, side = bank.shape[:4]
    channels = response.shape[0]
    length, strip, margin = 2 * side, tile_rows * side, side // 2
    entries = index.shape[1]
    blocks = tile_cols + 1
    low_count = 1 << ((wave_count.bit_length() - 1) // 2)
    high_count = wave_count // low_count
    slab = strip // wave_count
    factors = tables(side)
    dims = (tile_count, low_count, high_count, tile_rows, tile_cols, entries, side, waves, channels)
    smem = pl.BlockSpec(memory_space=pltpu.SMEM)
    vmem = pl.BlockSpec(memory_space=pltpu.VMEM)
    f32, bf16, sems = jnp.float32, jnp.bfloat16, pltpu.SemaphoreType.DMA
    tiles = tile_rows * waves
    planes = tile_rows * channels
    return pl.pallas_call(
        functools.partial(camera_kernel, dims),
        grid=(blocks + 3,),
        in_specs=[
            smem,
            smem,
            smem,
            vmem,
            vmem,
            vmem,
            vmem,
            pl.BlockSpec((waves, strip, side), lambda s: (0, 0, jnp.minimum(s, tile_cols - 1))),
            vmem,
        ],
        out_specs=vmem,
        out_shape=jax.ShapeDtypeStruct((channels, slab, tile_cols * side), f32),
        scratch_shapes=[
            pltpu.VMEM((tile_cols, waves, side, side), f32),
            pltpu.VMEM((tile_cols, waves, side, side), f32),
            pltpu.VMEM((planes * length, side), f32),
            pltpu.VMEM((tiles * length, length), bf16),
            pltpu.VMEM((tiles * length, length), bf16),
            pltpu.VMEM((planes * length, 3 * length), bf16),
            pltpu.VMEM((3 * length, planes * side), bf16),
            pltpu.VMEM((channels * slab, side), f32),
            pltpu.VMEM((blocks, channels, strip + side, side), f32),
            pltpu.VMEM((blocks, channels, margin, side), f32),
            pltpu.VMEM((blocks, channels, margin, side), f32),
            pltpu.VMEM((blocks, low_count, high_count, channels, slab, side), f32),
            pltpu.VMEM((blocks, low_count - 1, high_count, channels, slab, side), f32),
            pltpu.VMEM((blocks, high_count, channels, slab, side), f32),
            pltpu.VMEM((blocks, high_count - 1, channels, slab, side), f32),
            sems((2, tile_cols)),
            sems((2, tile_cols)),
            sems((2, blocks)),
            sems((2, blocks)),
            sems((blocks, low_count - 1)),
            sems((blocks, low_count - 1)),
            sems((blocks, high_count - 1)),
            sems((blocks, high_count - 1)),
        ],
        compiler_params=pltpu.CompilerParams(
            vmem_limit_bytes=VMEM_BYTES, collective_id=0, has_side_effects=True
        ),
        cost_estimate=pl.CostEstimate(
            flops=tile_cols * (tiles * 24 + planes * 36) * 2 * side**3,
            bytes_accessed=8 * waves * strip * tile_cols * side,
            transcendentals=0,
        ),
        name="camera",
    )(index, weights, response, *factors, scene, bank)


def per_device(scene, bank, psf_index, psf_weight, response):
    return camera(
        scene,
        bank,
        psf_index.transpose(0, 2, 1),
        psf_weight.transpose(0, 2, 1),
        response,
        lax.axis_size("tile"),
        lax.axis_size("wave"),
    )


def solution(mesh):
    in_specs = (
        P("wave", "tile", None),
        P("wave", "tile", None, None, None),
        P("tile", None, None),
        P("tile", None, None),
        P(),
    )
    out_specs = P(None, ("tile", "wave"), None)
    return jax.shard_map(
        per_device, mesh=mesh, in_specs=in_specs, out_specs=out_specs, check_vma=False
    )
```

```python
import functools

import jax
import jax.numpy as jnp
import ml_dtypes
import numpy as np
from jax import lax
from jax.experimental import pallas as pl
from jax.experimental.pallas import tpu as pltpu
from jax.sharding import PartitionSpec as P

CHUNK_ROWS = 16
VMEM_BYTES = 56 * 1024 * 1024


def halves(table):
    high = table.astype(ml_dtypes.bfloat16)
    low = (table - high.astype(np.float64)).astype(ml_dtypes.bfloat16)
    return high, low


def left_factor(table):
    high, low = halves(table)
    return np.concatenate([high, high, low], axis=1)


def right_factor(table):
    high, low = halves(table)
    return np.concatenate([high, high, low], axis=0)


def tables(side):
    length = 2 * side
    odd = 2 * np.arange(side)[:, None] + 1
    angle = np.pi * (odd * np.arange(length)[None, :] % (2 * length)) / length
    cosine, sine = np.cos(angle), np.sin(angle)
    rows_in = np.concatenate([cosine[:, :side], -sine[:, :side]], axis=0)
    cols_in = np.concatenate([cosine[:, :side].T, sine[:, :side].T], axis=1)
    cols_out = np.concatenate([cosine, sine], axis=0)
    rows_out = np.concatenate([cosine.T, -sine.T], axis=1) * (2.0 / (length * length))
    return left_factor(rows_in), right_factor(cols_in), right_factor(cols_out), left_factor(rows_out)


def split(values):
    high = values.astype(jnp.bfloat16)
    low = (values - high.astype(jnp.float32)).astype(jnp.bfloat16)
    return high, low


def dot(left, right):
    return jnp.dot(left, right, preferred_element_type=jnp.float32)


def put_rows(out_ref, values, side, lanes):
    high, low = split(values)
    out_ref[0:side, lanes] = high
    out_ref[side : 2 * side, lanes] = low
    out_ref[2 * side : 3 * side, lanes] = high


def lift(values):
    high, low = split(values)
    return [high, low, high]


def camera_kernel(
    dims,
    index_ref,
    weight_ref,
    response_ref,
    rows_in,
    cols_in,
    cols_out,
    rows_out,
    scene_ref,
    bank_ref,
    out_ref,
    own,
    above,
    below,
    carry,
    scene_mid,
    psf_mid,
    mixed,
    back,
    last,
    light,
    light_above,
    light_below,
    middle,
    got_low,
    part,
    got_high,
    bank_held,
    bank_sent,
    bank_got,
    light_sent,
    light_got,
    low_sent,
    low_got,
    high_sent,
    high_got,
):
    tile_count, low_count, high_count, tile_rows, tile_cols, entries, side, waves, channels = dims
    step = pl.program_id(0)
    length, margin, strip = 2 * side, side // 2, tile_rows * side
    slab = strip // (low_count * high_count)
    blocks = tile_cols + 1
    edge = margin * high_count // strip
    inner, outer = range(edge, high_count - edge), [*range(edge), *range(high_count - edge, high_count)]
    spans = ((edge, high_count - 2 * edge), (0, edge), (high_count - edge, edge))
    tile, wave = lax.axis_index("tile"), lax.axis_index("wave")
    low, high = lax.rem(wave, low_count), lax.div(wave, low_count)
    has_above, has_below = tile > 0, tile < tile_count - 1
    tile_above = lax.rem(tile + tile_count - 1, tile_count)
    tile_below = lax.rem(tile + 1, tile_count)

    def remote(src, dst, sent, got, axis, index):
        return pltpu.make_async_remote_copy(
            src_ref=src,
            dst_ref=dst,
            send_sem=sent,
            recv_sem=got,
            device_id={axis: index},
            device_id_type=pl.DeviceIdType.MESH,
        )

    def bank_own(c):
        return pltpu.make_async_copy(bank_ref.at[:, :, c], own.at[:, :, c], bank_held.at[c])

    def bank_down(c):
        return remote(
            bank_ref.at[:, tile_rows - 1, c], above.at[c], bank_sent.at[0, c], bank_got.at[0, c], "tile", tile_below
        )

    def bank_up(c):
        return remote(bank_ref.at[:, 0, c], below.at[c], bank_sent.at[1, c], bank_got.at[1, c], "tile", tile_above)

    def light_down(b):
        return remote(
            light.at[b, :, pl.ds(strip + margin, margin)],
            light_above.at[b],
            light_sent.at[0, b],
            light_got.at[0, b],
            "tile",
            tile_below,
        )

    def light_up(b):
        return remote(
            light.at[b, :, pl.ds(0, margin)], light_below.at[b], light_sent.at[1, b], light_got.at[1, b], "tile", tile_above
        )

    def start_pair(down, up):
        @pl.when(has_below)
        def _():
            down.start()

        @pl.when(has_above)
        def _():
            up.start()

    def wait_pair(down, up):
        @pl.when(has_below)
        def _():
            down.wait_send()
            up.wait_recv()

        @pl.when(has_above)
        def _():
            up.wait_send()
            down.wait_recv()

    def low_peer(d):
        return lax.rem(low + d, low_count)

    def high_peer(d):
        return lax.rem(high + d, high_count)

    def to_low(b, d, part_id):
        peer = low_peer(d)
        first, count = spans[part_id]
        return remote(
            middle.at[b, peer, pl.ds(first, count)],
            got_low.at[b, d - 1, pl.ds(first, count)],
            low_sent.at[b, d - 1, part_id],
            low_got.at[b, d - 1, part_id],
            "wave",
            high * low_count + peer,
        )

    def send_slabs(b, slabs, part_ids):
        for ch in range(channels):
            for h in slabs:
                for o in range(low_count):
                    start = (h * low_count + o) * slab
                    value = light[b, ch, margin + start : margin + start + slab, :]
                    if start < margin:
                        value = value + light_above[b, ch, start : start + slab, :]
                    if start >= strip - margin:
                        start = start - (strip - margin)
                        value = value + light_below[b, ch, start : start + slab, :]
                    middle[b, o, h, ch] = value
        for d in range(1, low_count):
            for part_id in part_ids:
                to_low(b, d, part_id).start()

    def sum_slabs(b, slabs, part_ids):
        for d in range(1, low_count):
            for part_id in part_ids:
                to_low(b, d, part_id).wait()
        for h in slabs:
            total = middle[b, low, h]
            for d in range(1, low_count):
                total = total + got_low[b, d - 1, h]
            part[b, h] = total
        for d in range(1, high_count):
            peer = high_peer(d)
            is_inner = jnp.logical_and(peer >= edge, peer < high_count - edge)

            @pl.when(is_inner if slabs is inner else jnp.logical_not(is_inner))
            def _():
                to_high(b, d).start()

    def to_high(b, d):
        peer = high_peer(d)
        return remote(
            part.at[b, peer],
            got_high.at[b, d - 1],
            high_sent.at[b, d - 1],
            high_got.at[b, d - 1],
            "wave",
            peer * low_count + low,
        )

    @pl.when(step == 0)
    def _():
        barrier = pltpu.get_barrier_semaphore()

        def greet(axis, index):
            pl.semaphore_signal(barrier, inc=1, device_id={axis: index}, device_id_type=pl.DeviceIdType.MESH)

        for d in range(1, low_count):
            greet("wave", high * low_count + low_peer(d))
        for d in range(1, high_count):
            greet("wave", high_peer(d) * low_count + low)

        @pl.when(has_above)
        def _():
            greet("tile", tile_above)

        @pl.when(has_below)
        def _():
            greet("tile", tile_below)

        others = low_count + high_count - 2
        pl.semaphore_wait(barrier, others + has_above.astype(jnp.int32) + has_below.astype(jnp.int32))
        for c in range(2):
            start_pair(bank_down(c), bank_up(c))
        for c in range(tile_cols):
            bank_own(c).start()
        carry[...] = jnp.zeros_like(carry)

        @pl.when(jnp.logical_not(has_above))
        def _():
            above[...] = jnp.zeros_like(above)
            light_above[...] = jnp.zeros_like(light_above)

        @pl.when(jnp.logical_not(has_below))
        def _():
            below[...] = jnp.zeros_like(below)
            light_below[...] = jnp.zeros_like(light_below)

    def transform_rows(mid, fields, t):
        pair = [jnp.concatenate(lift(field), axis=0) for field in (fields(t), fields(t + 1))]
        first = dot(rows_in[...], jnp.concatenate(pair, axis=1))
        for j in range(2):
            upper_bits, lower_bits = split(first[:, j * side : (j + 1) * side])
            rows = slice((t + j) * length, (t + j + 1) * length)
            mid[rows, 0:side] = upper_bits
            mid[rows, side:length] = lower_bits

    def scene_field(t):
        r, w = divmod(t, waves)
        return scene_ref[w, r * side : (r + 1) * side, :]

    tiles = tile_rows * waves

    @pl.when(step < tile_cols)
    def _():
        col = step
        for t in range(0, tiles, 2):
            transform_rows(scene_mid, scene_field, t)

        @pl.when(step == 0)
        def _():
            bank_own(0).wait()
            wait_pair(bank_down(0), bank_up(0))

        @pl.when(step + 1 < tile_cols)
        def _():
            bank_own(step + 1).wait()
            wait_pair(bank_down(step + 1), bank_up(step + 1))

        @pl.when(step + 2 < tile_cols)
        def _():
            start_pair(bank_down(step + 2), bank_up(step + 2))

        near = (jnp.maximum(col - 1, 0), col, jnp.minimum(col + 1, tile_cols - 1))
        shares = []
        for r in range(tile_rows):
            here = (tile * tile_rows + r) * tile_cols + col
            listed = [(index_ref[r, k, col] - here, weight_ref[r, k, col]) for k in range(entries)]
            for i in range(3):
                for j in range(3):
                    offset = (i - 1) * tile_cols + j - 1
                    share = sum(jnp.where(away == offset, weight, 0) for away, weight in listed)
                    shares.append(share.astype(jnp.float32) * (1.0 / 65536.0))

        def psf_field(t):
            r, w = divmod(t, waves)
            psf = None
            for i in range(3):
                for j in range(3):
                    row = r + i - 1
                    if row < 0:
                        field = above[near[j], w]
                    elif row >= tile_rows:
                        field = below[near[j], w]
                    else:
                        field = own[w, row, near[j]]
                    term = shares[9 * r + 3 * i + j] * field
                    psf = term if psf is None else psf + term
            return psf

        for t in range(0, tiles, 2):
            transform_rows(psf_mid, psf_field, t)

        def some_rows(r, index):
            start = index * CHUNK_ROWS
            lines = []
            for w in range(waves):
                top = start + (r * waves + w) * length
                for mid in (scene_mid, psf_mid):
                    for first in (top, top + side):
                        both = mid[first : first + CHUNK_ROWS, :]
                        lines.append(jnp.concatenate([both, both[:, 0:side]], axis=1))
            spec = dot(jnp.concatenate(lines, axis=0), cols_in[...])

            def quarters(block):
                top = block * 2 * CHUNK_ROWS
                upper, lower = slice(top, top + CHUNK_ROWS), slice(top + CHUNK_ROWS, top + 2 * CHUNK_ROWS)
                a, b, d, e = spec[upper, :side], spec[upper, side:], spec[lower, :side], spec[lower, side:]
                return a + e, d - b, a - e, d + b

            sums = [None] * channels
            for w in range(waves):
                s1r, s1i, s2r, s2i = quarters(2 * w)
                p1r, p1i, p2r, p2i = quarters(2 * w + 1)
                q1r, q1i = s1r * p1r - s1i * p1i, s1r * p1i + s1i * p1r
                q2r, q2i = s2r * p2r - s2i * p2i, s2r * p2i + s2i * p2r
                parts = (q1r + q2r, q2i - q1i, q1i + q2i, q1r - q2r)
                for ch in range(channels):
                    gain = response_ref[ch, wave * waves + w]
                    terms = [gain * value for value in parts]
                    sums[ch] = terms if w == 0 else [old + new for old, new in zip(sums[ch], terms)]
            for ch in range(channels):
                top = start + (r * channels + ch) * length
                for j, rows in ((0, pl.ds(top, CHUNK_ROWS)), (2, pl.ds(top + side, CHUNK_ROWS))):
                    for h in range(2):
                        upper_bits, lower_bits = split(sums[ch][j + h])
                        mixed[rows, h * side : (h + 1) * side] = upper_bits
                        mixed[rows, length + h * side : length + (h + 1) * side] = lower_bits
                        mixed[rows, 2 * length + h * side : 2 * length + (h + 1) * side] = upper_bits

        for r in range(tile_rows):
            for index in range(side // CHUNK_ROWS):
                some_rows(r, index)
            planes = slice(r * channels * length, (r + 1) * channels * length)
            partial = dot(mixed[planes, :], cols_out[...])
            for ch in range(channels):
                rows = slice((r * channels + ch) * length, (r * channels + ch + 1) * length)
                lane = (r * channels + ch) * side
                block = partial[ch * length : (ch + 1) * length, :]
                put_rows(back, block[:, 0:side] + carry[rows, :], length, slice(lane, lane + side))
                carry[rows, :] = block[:, side:length]

    @pl.when(step == tile_cols)
    def _():
        for r in range(tile_rows):
            for ch in range(channels):
                rows = slice((r * channels + ch) * length, (r * channels + ch + 1) * length)
                lane = (r * channels + ch) * side
                put_rows(back, carry[rows, :], length, slice(lane, lane + side))

    @pl.when(step < blocks)
    def _():
        now = step
        rays = dot(rows_out[...], back[...])
        for ch in range(channels):
            for r in range(tile_rows + 1):
                total = None
                if r < tile_rows:
                    lane = (r * channels + ch) * side
                    total = rays[0:side, lane : lane + side]
                if r > 0:
                    lane = ((r - 1) * channels + ch) * side
                    tail = rays[side:length, lane : lane + side]
                    total = tail if total is None else total + tail
                light[now, ch, r * side : (r + 1) * side, :] = total
        start_pair(light_down(now), light_up(now))
        send_slabs(now, inner, (0,))

    @pl.when(jnp.logical_and(step >= 1, step < blocks + 1))
    def _():
        b = step - 1
        wait_pair(light_down(b), light_up(b))
        send_slabs(b, outer, (1, 2))
        sum_slabs(b, inner, (0,))

    @pl.when(jnp.logical_and(step >= 2, step < blocks + 2))
    def _():
        sum_slabs(step - 2, outer, (1, 2))

    @pl.when(step >= 3)
    def _():
        b = step - 3
        for d in range(1, high_count):
            to_high(b, d).wait()
        total = part[b, high]
        for d in range(1, high_count):
            total = total + got_high[b, d - 1]
        turned = pltpu.roll(total.reshape(channels * slab, side), margin, 1)

        @pl.when(b > 0)
        def _():
            is_left = lax.broadcasted_iota(jnp.int32, turned.shape, 1) < margin
            whole = jnp.where(is_left, last[...], turned).reshape(channels, slab, side)
            out_ref[:, :, pl.ds(pl.multiple_of((b - 1) * side, side), side)] = whole

        last[...] = turned


def camera(scene, bank, index, weights, response, tile_count, wave_count):
    waves, tile_rows, tile_cols, side = bank.shape[:4]
    channels = response.shape[0]
    length, strip, margin = 2 * side, tile_rows * side, side // 2
    entries = index.shape[1]
    blocks = tile_cols + 1
    low_count = 1 << ((wave_count.bit_length() - 1) // 2)
    high_count = wave_count // low_count
    slab = strip // wave_count
    factors = tables(side)
    dims = (tile_count, low_count, high_count, tile_rows, tile_cols, entries, side, waves, channels)
    smem = pl.BlockSpec(memory_space=pltpu.SMEM)
    vmem = pl.BlockSpec(memory_space=pltpu.VMEM)
    f32, bf16, sems = jnp.float32, jnp.bfloat16, pltpu.SemaphoreType.DMA
    tiles = tile_rows * waves
    planes = tile_rows * channels
    return pl.pallas_call(
        functools.partial(camera_kernel, dims),
        grid=(blocks + 3,),
        in_specs=[
            smem,
            smem,
            smem,
            vmem,
            vmem,
            vmem,
            vmem,
            pl.BlockSpec((waves, strip, side), lambda s: (0, 0, jnp.minimum(s, tile_cols - 1))),
            pl.BlockSpec(memory_space=pl.ANY),
        ],
        out_specs=vmem,
        out_shape=jax.ShapeDtypeStruct((channels, slab, tile_cols * side), f32),
        scratch_shapes=[
            pltpu.VMEM(bank.shape, f32),
            pltpu.VMEM((tile_cols, waves, side, side), f32),
            pltpu.VMEM((tile_cols, waves, side, side), f32),
            pltpu.VMEM((planes * length, side), f32),
            pltpu.VMEM((tiles * length, length), bf16),
            pltpu.VMEM((tiles * length, length), bf16),
            pltpu.VMEM((planes * length, 3 * length), bf16),
            pltpu.VMEM((3 * length, planes * side), bf16),
            pltpu.VMEM((channels * slab, side), f32),
            pltpu.VMEM((blocks, channels, strip + side, side), f32),
            pltpu.VMEM((blocks, channels, margin, side), f32),
            pltpu.VMEM((blocks, channels, margin, side), f32),
            pltpu.VMEM((blocks, low_count, high_count, channels, slab, side), f32),
            pltpu.VMEM((blocks, low_count - 1, high_count, channels, slab, side), f32),
            pltpu.VMEM((blocks, high_count, channels, slab, side), f32),
            pltpu.VMEM((blocks, high_count - 1, channels, slab, side), f32),
            sems((tile_cols,)),
            sems((2, tile_cols)),
            sems((2, tile_cols)),
            sems((2, blocks)),
            sems((2, blocks)),
            sems((blocks, low_count - 1, 3)),
            sems((blocks, low_count - 1, 3)),
            sems((blocks, high_count - 1)),
            sems((blocks, high_count - 1)),
        ],
        compiler_params=pltpu.CompilerParams(
            vmem_limit_bytes=VMEM_BYTES, collective_id=0, has_side_effects=True
        ),
        cost_estimate=pl.CostEstimate(
            flops=tile_cols * (tiles * 24 + planes * 36) * 2 * side**3,
            bytes_accessed=8 * waves * strip * tile_cols * side,
            transcendentals=0,
        ),
        name="camera",
    )(index, weights, response, *factors, scene, bank)


def per_device(scene, bank, psf_index, psf_weight, response):
    return camera(
        scene,
        bank,
        psf_index.transpose(0, 2, 1),
        psf_weight.transpose(0, 2, 1),
        response,
        lax.axis_size("tile"),
        lax.axis_size("wave"),
    )


def solution(mesh):
    in_specs = (
        P("wave", "tile", None),
        P("wave", "tile", None, None, None),
        P("tile", None, None),
        P("tile", None, None),
        P(),
    )
    out_specs = P(None, ("tile", "wave"), None)
    return jax.shard_map(
        per_device, mesh=mesh, in_specs=in_specs, out_specs=out_specs, check_vma=False
    )
```

```python
import functools

import jax
import jax.numpy as jnp
import ml_dtypes
import numpy as np
from jax import lax
from jax.experimental import pallas as pl
from jax.experimental.pallas import tpu as pltpu
from jax.sharding import PartitionSpec as P

CHUNK_ROWS = 16
VMEM_BYTES = 56 * 1024 * 1024


def halves(table):
    high = table.astype(ml_dtypes.bfloat16)
    low = (table - high.astype(np.float64)).astype(ml_dtypes.bfloat16)
    return high, low


def left_factor(table):
    high, low = halves(table)
    return np.concatenate([high, high, low], axis=1)


def stacked_factor(table):
    high, low = halves(table)
    top = np.concatenate([high, high], axis=1)
    return np.concatenate([top, np.concatenate([low, np.zeros_like(low)], axis=1)], axis=0)


def right_factor(table):
    high, low = halves(table)
    return np.concatenate([high, high, low], axis=0)


def tables(side):
    length = 2 * side
    odd = 2 * np.arange(side)[:, None] + 1
    angle = np.pi * (odd * np.arange(length)[None, :] % (2 * length)) / length
    cosine, sine = np.cos(angle), np.sin(angle)
    rows_in = np.concatenate([cosine[:, :side], -sine[:, :side]], axis=0)
    cols_in = np.concatenate([cosine[:, :side].T, sine[:, :side].T], axis=1)
    cols_out = np.concatenate([cosine, sine], axis=0)
    rows_out = np.concatenate([cosine.T, -sine.T], axis=1) * (2.0 / (length * length))
    return stacked_factor(rows_in), right_factor(cols_in), right_factor(cols_out), left_factor(rows_out)


def split(values):
    high = values.astype(jnp.bfloat16)
    low = (values - high.astype(jnp.float32)).astype(jnp.bfloat16)
    return high, low


def dot(left, right):
    return jnp.dot(left, right, preferred_element_type=jnp.float32)


def put_rows(out_ref, values, side, lanes):
    high, low = split(values)
    out_ref[0:side, lanes] = high
    out_ref[side : 2 * side, lanes] = low
    out_ref[2 * side : 3 * side, lanes] = high


def camera_kernel(
    dims,
    index_ref,
    weight_ref,
    response_ref,
    rows_in,
    cols_in,
    cols_out,
    rows_out,
    scene_ref,
    bank_ref,
    out_ref,
    own,
    above,
    below,
    carry,
    scene_mid,
    psf_mid,
    mixed,
    back,
    last,
    light,
    light_above,
    light_below,
    middle,
    got_low,
    part,
    got_high,
    bank_held,
    bank_sent,
    bank_got,
    light_sent,
    light_got,
    low_sent,
    low_got,
    high_sent,
    high_got,
):
    tile_count, low_count, high_count, tile_rows, tile_cols, entries, side, waves, channels = dims
    step = pl.program_id(0)
    length, margin, strip = 2 * side, side // 2, tile_rows * side
    slab = strip // (low_count * high_count)
    blocks = tile_cols + 1
    edge = margin * high_count // strip
    inner, outer = range(edge, high_count - edge), [*range(edge), *range(high_count - edge, high_count)]
    spans = ((edge, high_count - 2 * edge), (0, edge), (high_count - edge, edge))
    tile, wave = lax.axis_index("tile"), lax.axis_index("wave")
    low, high = lax.rem(wave, low_count), lax.div(wave, low_count)
    has_above, has_below = tile > 0, tile < tile_count - 1
    tile_above = lax.rem(tile + tile_count - 1, tile_count)
    tile_below = lax.rem(tile + 1, tile_count)

    def remote(src, dst, sent, got, axis, index):
        return pltpu.make_async_remote_copy(
            src_ref=src,
            dst_ref=dst,
            send_sem=sent,
            recv_sem=got,
            device_id={axis: index},
            device_id_type=pl.DeviceIdType.MESH,
        )

    def bank_own(c):
        return pltpu.make_async_copy(bank_ref.at[:, :, c], own.at[:, :, c], bank_held.at[c])

    def bank_down(c):
        return remote(
            bank_ref.at[:, tile_rows - 1, c], above.at[c], bank_sent.at[0, c], bank_got.at[0, c], "tile", tile_below
        )

    def bank_up(c):
        return remote(bank_ref.at[:, 0, c], below.at[c], bank_sent.at[1, c], bank_got.at[1, c], "tile", tile_above)

    def light_down(b):
        return remote(
            light.at[b, :, pl.ds(strip + margin, margin)],
            light_above.at[b],
            light_sent.at[0, b],
            light_got.at[0, b],
            "tile",
            tile_below,
        )

    def light_up(b):
        return remote(
            light.at[b, :, pl.ds(0, margin)], light_below.at[b], light_sent.at[1, b], light_got.at[1, b], "tile", tile_above
        )

    def start_pair(down, up):
        @pl.when(has_below)
        def _():
            down.start()

        @pl.when(has_above)
        def _():
            up.start()

    def wait_pair(down, up):
        @pl.when(has_below)
        def _():
            down.wait_send()
            up.wait_recv()

        @pl.when(has_above)
        def _():
            up.wait_send()
            down.wait_recv()

    def low_peer(d):
        return lax.rem(low + d, low_count)

    def high_peer(d):
        return lax.rem(high + d, high_count)

    def to_low(b, d, part_id):
        peer = low_peer(d)
        first, count = spans[part_id]
        return remote(
            middle.at[b, peer, pl.ds(first, count)],
            got_low.at[b, d - 1, pl.ds(first, count)],
            low_sent.at[b, d - 1, part_id],
            low_got.at[b, d - 1, part_id],
            "wave",
            high * low_count + peer,
        )

    def send_slabs(b, slabs, part_ids):
        for ch in range(channels):
            for h in slabs:
                for o in range(low_count):
                    start = (h * low_count + o) * slab
                    value = light[b, ch, margin + start : margin + start + slab, :]
                    if start < margin:
                        value = value + light_above[b, ch, start : start + slab, :]
                    if start >= strip - margin:
                        start = start - (strip - margin)
                        value = value + light_below[b, ch, start : start + slab, :]
                    middle[b, o, h, ch] = value
        for d in range(1, low_count):
            for part_id in part_ids:
                to_low(b, d, part_id).start()

    def sum_slabs(b, slabs, part_ids):
        for d in range(1, low_count):
            for part_id in part_ids:
                to_low(b, d, part_id).wait()
        for h in slabs:
            total = middle[b, low, h]
            for d in range(1, low_count):
                total = total + got_low[b, d - 1, h]
            part[b, h] = total
        for d in range(1, high_count):
            peer = high_peer(d)
            is_inner = jnp.logical_and(peer >= edge, peer < high_count - edge)

            @pl.when(is_inner if slabs is inner else jnp.logical_not(is_inner))
            def _():
                to_high(b, d).start()

    def to_high(b, d):
        peer = high_peer(d)
        return remote(
            part.at[b, peer],
            got_high.at[b, d - 1],
            high_sent.at[b, d - 1],
            high_got.at[b, d - 1],
            "wave",
            peer * low_count + low,
        )

    @pl.when(step == 0)
    def _():
        barrier = pltpu.get_barrier_semaphore()

        def greet(axis, index):
            pl.semaphore_signal(barrier, inc=1, device_id={axis: index}, device_id_type=pl.DeviceIdType.MESH)

        for d in range(1, low_count):
            greet("wave", high * low_count + low_peer(d))
        for d in range(1, high_count):
            greet("wave", high_peer(d) * low_count + low)

        @pl.when(has_above)
        def _():
            greet("tile", tile_above)

        @pl.when(has_below)
        def _():
            greet("tile", tile_below)

        others = low_count + high_count - 2
        pl.semaphore_wait(barrier, others + has_above.astype(jnp.int32) + has_below.astype(jnp.int32))
        for c in range(2):
            start_pair(bank_down(c), bank_up(c))
        for c in range(tile_cols):
            bank_own(c).start()
        carry[...] = jnp.zeros_like(carry)

        @pl.when(jnp.logical_not(has_above))
        def _():
            above[...] = jnp.zeros_like(above)
            light_above[...] = jnp.zeros_like(light_above)

        @pl.when(jnp.logical_not(has_below))
        def _():
            below[...] = jnp.zeros_like(below)
            light_below[...] = jnp.zeros_like(light_below)

    def transform_rows(mid, fields, t):
        pair = [jnp.concatenate(split(field), axis=0) for field in (fields(t), fields(t + 1))]
        first = dot(rows_in[...], jnp.concatenate(pair, axis=1))
        first = first[:length] + first[length:]
        for j in range(2):
            upper_bits, lower_bits = split(first[:, j * side : (j + 1) * side])
            rows = slice((t + j) * length, (t + j + 1) * length)
            mid[rows, 0:side] = upper_bits
            mid[rows, side:length] = lower_bits

    def scene_field(t):
        r, w = divmod(t, waves)
        return scene_ref[w, r * side : (r + 1) * side, :]

    tiles = tile_rows * waves

    @pl.when(step < tile_cols)
    def _():
        col = step
        for t in range(0, tiles, 2):
            transform_rows(scene_mid, scene_field, t)

        @pl.when(step == 0)
        def _():
            bank_own(0).wait()
            wait_pair(bank_down(0), bank_up(0))

        @pl.when(step + 1 < tile_cols)
        def _():
            bank_own(step + 1).wait()
            wait_pair(bank_down(step + 1), bank_up(step + 1))

        @pl.when(step + 2 < tile_cols)
        def _():
            start_pair(bank_down(step + 2), bank_up(step + 2))

        near = (jnp.maximum(col - 1, 0), col, jnp.minimum(col + 1, tile_cols - 1))
        shares = []
        for r in range(tile_rows):
            here = (tile * tile_rows + r) * tile_cols + col
            listed = [(index_ref[r, k, col] - here, weight_ref[r, k, col]) for k in range(entries)]
            for i in range(3):
                for j in range(3):
                    offset = (i - 1) * tile_cols + j - 1
                    share = sum(jnp.where(away == offset, weight, 0) for away, weight in listed)
                    shares.append(share.astype(jnp.float32) * (1.0 / 65536.0))

        def psf_field(t):
            r, w = divmod(t, waves)
            psf = None
            for i in range(3):
                for j in range(3):
                    row = r + i - 1
                    if row < 0:
                        field = above[near[j], w]
                    elif row >= tile_rows:
                        field = below[near[j], w]
                    else:
                        field = own[w, row, near[j]]
                    term = shares[9 * r + 3 * i + j] * field
                    psf = term if psf is None else psf + term
            return psf

        for t in range(0, tiles, 2):
            transform_rows(psf_mid, psf_field, t)

        def some_rows(r, index):
            start = index * CHUNK_ROWS
            lines = []
            for w in range(waves):
                top = start + (r * waves + w) * length
                for mid in (scene_mid, psf_mid):
                    for first in (top, top + side):
                        both = mid[first : first + CHUNK_ROWS, :]
                        lines.append(jnp.concatenate([both, both[:, 0:side]], axis=1))
            spec = dot(jnp.concatenate(lines, axis=0), cols_in[...])

            def quarters(block):
                top = block * 2 * CHUNK_ROWS
                upper, lower = slice(top, top + CHUNK_ROWS), slice(top + CHUNK_ROWS, top + 2 * CHUNK_ROWS)
                a, b, d, e = spec[upper, :side], spec[upper, side:], spec[lower, :side], spec[lower, side:]
                return a + e, d - b, a - e, d + b

            sums = [None] * channels
            for w in range(waves):
                s1r, s1i, s2r, s2i = quarters(2 * w)
                p1r, p1i, p2r, p2i = quarters(2 * w + 1)
                q1r, q1i = s1r * p1r - s1i * p1i, s1r * p1i + s1i * p1r
                q2r, q2i = s2r * p2r - s2i * p2i, s2r * p2i + s2i * p2r
                parts = (q1r + q2r, q2i - q1i, q1i + q2i, q1r - q2r)
                for ch in range(channels):
                    gain = response_ref[ch, wave * waves + w]
                    terms = [gain * value for value in parts]
                    sums[ch] = terms if w == 0 else [old + new for old, new in zip(sums[ch], terms)]
            for ch in range(channels):
                top = start + (r * channels + ch) * length
                for j, rows in ((0, pl.ds(top, CHUNK_ROWS)), (2, pl.ds(top + side, CHUNK_ROWS))):
                    for h in range(2):
                        upper_bits, lower_bits = split(sums[ch][j + h])
                        mixed[rows, h * side : (h + 1) * side] = upper_bits
                        mixed[rows, length + h * side : length + (h + 1) * side] = lower_bits
                        mixed[rows, 2 * length + h * side : 2 * length + (h + 1) * side] = upper_bits

        for r in range(tile_rows):
            for index in range(side // CHUNK_ROWS):
                some_rows(r, index)
            planes = slice(r * channels * length, (r + 1) * channels * length)
            partial = dot(mixed[planes, :], cols_out[...])
            for ch in range(channels):
                rows = slice((r * channels + ch) * length, (r * channels + ch + 1) * length)
                lane = (r * channels + ch) * side
                block = partial[ch * length : (ch + 1) * length, :]
                put_rows(back, block[:, 0:side] + carry[rows, :], length, slice(lane, lane + side))
                carry[rows, :] = block[:, side:length]

    @pl.when(step == tile_cols)
    def _():
        for r in range(tile_rows):
            for ch in range(channels):
                rows = slice((r * channels + ch) * length, (r * channels + ch + 1) * length)
                lane = (r * channels + ch) * side
                put_rows(back, carry[rows, :], length, slice(lane, lane + side))

    @pl.when(step < blocks)
    def _():
        now = step
        rays = dot(rows_out[...], back[...])
        for ch in range(channels):
            for r in range(tile_rows + 1):
                total = None
                if r < tile_rows:
                    lane = (r * channels + ch) * side
                    total = rays[0:side, lane : lane + side]
                if r > 0:
                    lane = ((r - 1) * channels + ch) * side
                    tail = rays[side:length, lane : lane + side]
                    total = tail if total is None else total + tail
                light[now, ch, r * side : (r + 1) * side, :] = total
        start_pair(light_down(now), light_up(now))
        send_slabs(now, inner, (0,))

    @pl.when(jnp.logical_and(step >= 1, step < blocks + 1))
    def _():
        b = step - 1
        wait_pair(light_down(b), light_up(b))
        send_slabs(b, outer, (1, 2))
        sum_slabs(b, inner, (0,))

    @pl.when(jnp.logical_and(step >= 2, step < blocks + 2))
    def _():
        sum_slabs(step - 2, outer, (1, 2))

    @pl.when(step >= 3)
    def _():
        b = step - 3
        for d in range(1, high_count):
            to_high(b, d).wait()
        total = part[b, high]
        for d in range(1, high_count):
            total = total + got_high[b, d - 1]
        turned = pltpu.roll(total.reshape(channels * slab, side), margin, 1)

        @pl.when(b > 0)
        def _():
            is_left = lax.broadcasted_iota(jnp.int32, turned.shape, 1) < margin
            whole = jnp.where(is_left, last[...], turned).reshape(channels, slab, side)
            out_ref[:, :, pl.ds(pl.multiple_of((b - 1) * side, side), side)] = whole

        last[...] = turned


def camera(scene, bank, index, weights, response, tile_count, wave_count):
    waves, tile_rows, tile_cols, side = bank.shape[:4]
    channels = response.shape[0]
    length, strip, margin = 2 * side, tile_rows * side, side // 2
    entries = index.shape[1]
    blocks = tile_cols + 1
    low_count = 1 << ((wave_count.bit_length() - 1) // 2)
    high_count = wave_count // low_count
    slab = strip // wave_count
    factors = tables(side)
    dims = (tile_count, low_count, high_count, tile_rows, tile_cols, entries, side, waves, channels)
    smem = pl.BlockSpec(memory_space=pltpu.SMEM)
    vmem = pl.BlockSpec(memory_space=pltpu.VMEM)
    f32, bf16, sems = jnp.float32, jnp.bfloat16, pltpu.SemaphoreType.DMA
    tiles = tile_rows * waves
    planes = tile_rows * channels
    return pl.pallas_call(
        functools.partial(camera_kernel, dims),
        grid=(blocks + 3,),
        in_specs=[
            smem,
            smem,
            smem,
            vmem,
            vmem,
            vmem,
            vmem,
            pl.BlockSpec((waves, strip, side), lambda s: (0, 0, jnp.minimum(s, tile_cols - 1))),
            pl.BlockSpec(memory_space=pl.ANY),
        ],
        out_specs=vmem,
        out_shape=jax.ShapeDtypeStruct((channels, slab, tile_cols * side), f32),
        scratch_shapes=[
            pltpu.VMEM(bank.shape, f32),
            pltpu.VMEM((tile_cols, waves, side, side), f32),
            pltpu.VMEM((tile_cols, waves, side, side), f32),
            pltpu.VMEM((planes * length, side), f32),
            pltpu.VMEM((tiles * length, length), bf16),
            pltpu.VMEM((tiles * length, length), bf16),
            pltpu.VMEM((planes * length, 3 * length), bf16),
            pltpu.VMEM((3 * length, planes * side), bf16),
            pltpu.VMEM((channels * slab, side), f32),
            pltpu.VMEM((blocks, channels, strip + side, side), f32),
            pltpu.VMEM((blocks, channels, margin, side), f32),
            pltpu.VMEM((blocks, channels, margin, side), f32),
            pltpu.VMEM((blocks, low_count, high_count, channels, slab, side), f32),
            pltpu.VMEM((blocks, low_count - 1, high_count, channels, slab, side), f32),
            pltpu.VMEM((blocks, high_count, channels, slab, side), f32),
            pltpu.VMEM((blocks, high_count - 1, channels, slab, side), f32),
            sems((tile_cols,)),
            sems((2, tile_cols)),
            sems((2, tile_cols)),
            sems((2, blocks)),
            sems((2, blocks)),
            sems((blocks, low_count - 1, 3)),
            sems((blocks, low_count - 1, 3)),
            sems((blocks, high_count - 1)),
            sems((blocks, high_count - 1)),
        ],
        compiler_params=pltpu.CompilerParams(
            vmem_limit_bytes=VMEM_BYTES, collective_id=0, has_side_effects=True
        ),
        cost_estimate=pl.CostEstimate(
            flops=tile_cols * (tiles * 24 + planes * 36) * 2 * side**3,
            bytes_accessed=8 * waves * strip * tile_cols * side,
            transcendentals=0,
        ),
        name="camera",
    )(index, weights, response, *factors, scene, bank)


def per_device(scene, bank, psf_index, psf_weight, response):
    return camera(
        scene,
        bank,
        psf_index.transpose(0, 2, 1),
        psf_weight.transpose(0, 2, 1),
        response,
        lax.axis_size("tile"),
        lax.axis_size("wave"),
    )


def solution(mesh):
    in_specs = (
        P("wave", "tile", None),
        P("wave", "tile", None, None, None),
        P("tile", None, None),
        P("tile", None, None),
        P(),
    )
    out_specs = P(None, ("tile", "wave"), None)
    return jax.shard_map(
        per_device, mesh=mesh, in_specs=in_specs, out_specs=out_specs, check_vma=False
    )
```
